512 devices in a mesh: leaf: 32 (over y_hi, z), grid: 16 (over x, y_lo, core).
Axes of the slice: x: 4, y: 4 (y_hi: 2, y_lo: 2; y = y_hi * 2 + y_lo), z: 16, core: 2. Of those that a mesh axis runs over, the one named last changes fastest.
Arguments:
- samples: bfloat16 [32, 512, 1024], P('leaf', 'grid'), may hold values from -6 to 6
- omega: bfloat16 [32, 512, 1024], P('leaf', 'grid'), may hold values from -6 to 6
- points: bfloat16 [8, 32, 512], P(None, 'leaf', 'grid'), may hold values from -5 to 5
- ranks: int32 [3, 32], replicated, may hold values from 256 to 512, as said below
- pivots: int32 [2, 32, 512], P(None, 'leaf'), may hold values from 0 to 1023, as said below
Outputs:
- top_samples: bfloat16 [32, 512, 1024], P('leaf', 'grid')
The draws below stay inside these ranges and needn't reach their ends.
Inputs may be any that keep to these rules, and one draw needn't show every extreme that they name: `ranks`: equal for all groups under one node. At every level, some node has rank 512 and some node has rank half of 512. `pivots`: rows of the two stacked children (below 512: first child; 512 and up: second child); within one list distinct, and each below its child's rank; equal for all groups under one parent.
All inputs are finite; a program needn't handle non-finite values.
Results may differ from the reference program's by a relative error of at most 0.0038.
Values may be sent and summed in bfloat16 or wider, within the bound.
A program may use at most 64 MiB of HBM per device.

```python
import jax
import jax.numpy as jnp
from jax import lax

R = 512
NS = 1024
PDIM = 8
LEVELS = 2
GROUPS = 32


def node_ranks(key):
    tiers = []
    for height in range(LEVELS + 1):
        nodes = GROUPS // 2 ** height
        node_draw = jax.random.randint(jax.random.fold_in(key, 100 + height), (nodes,), R // 2, R + 1)
        node_draw = node_draw.at[0].set(R).at[1].set(R // 2)
        tiers.append(jnp.repeat(node_draw, 2 ** height))
    return jnp.stack(tiers).astype(jnp.int32)


def draw_ranks(key, part):
    shared = node_ranks(key)
    return shared


def draw_pivots(key, part):
    shared = node_ranks(key)
    key = jax.random.fold_in(key, 5)
    tiers = []
    stacked = jnp.arange(2 * R, dtype=jnp.int32)
    for height in range(LEVELS):
        parents = GROUPS // 2 ** (height + 1)
        child_rank = shared[height, ::2 ** height].reshape(parents, 2)
        keys = jax.random.split(jax.random.fold_in(key, height), parents)
        scores = jax.vmap(lambda one: jax.random.permutation(one, 2 * R))(keys).astype(jnp.int32)
        alive = jnp.where(stacked[None, :] < R, stacked[None, :] < child_rank[:, :1], stacked[None, :] - R < child_rank[:, 1:])
        scores = scores + jnp.where(alive, 0, 4 * R).astype(jnp.int32)
        ranking = jnp.argsort(scores, axis=1, stable=True)[:, :R].astype(jnp.int32)
        tiers.append(jnp.repeat(ranking, 2 ** (height + 1), axis=0))
    return jnp.stack(tiers).astype(jnp.int32)


def block_scale(stream_key, dims, cuts, least, largest):
    def one(dim, shards_of):
        steps = jax.random.uniform(jax.random.fold_in(jax.random.fold_in(stream_key, 6), dim), (shards_of,), jnp.float32, least / len(cuts), largest / len(cuts))
        return jnp.repeat(jnp.exp(steps), dims[dim] // shards_of).reshape((-1,) + (1,) * (len(dims) - dim - 1))

    factor_of = one(*cuts[0])
    for cut in cuts[1:]:
        factor_of = factor_of * one(*cut)
    return factor_of


def normal_values(key, extent, width, most, cuts=(), held_as=jnp.bfloat16):
    entries = width * jax.random.normal(key, extent, jnp.float32)
    if cuts:
        entries = entries * block_scale(key, extent, cuts, -0.22, 0.18)
    return jnp.clip(entries, -most, most).astype(held_as)


def setup_inputs(seed: int = 0) -> dict:
    key_list = jax.random.split(jax.random.key(seed), 6)
    samples = normal_values(key_list[0], (GROUPS, R, NS), 1.0, 6.0, ((0, 32), (1, 16)))
    omega = normal_values(key_list[1], (GROUPS, R, NS), 1.0, 6.0, ((0, 32), (1, 16)))
    points = normal_values(key_list[2], (PDIM, GROUPS, R), 1.0, 5.0, ((1, 32), (2, 16)))
    ranks = draw_ranks(jax.random.fold_in(key_list[5], 71), 0)
    pivots = draw_pivots(jax.random.fold_in(key_list[5], 71), 0)
    return {"samples": samples, "omega": omega, "points": points, "ranks": ranks, "pivots": pivots}


kernel_rate = 0.6
ridge_shift = 1.0


def kernel_block(left, right, left_ids):
    distance = jnp.zeros((left.shape[1], right.shape[1]), jnp.float32)
    for component in range(left.shape[0]):
        spread = left[component].astype(jnp.float32)[:, None] - right[component].astype(jnp.float32)[None, :]
        distance = distance + spread * spread
    column_ids = jnp.arange(right.shape[1], dtype=jnp.int32)
    diagonal = (left_ids[:, None] == column_ids[None, :]).astype(jnp.float32)
    return (jnp.exp(-kernel_rate * distance) + ridge_shift * diagonal).astype(jnp.bfloat16)


def reference(samples, omega, points, ranks, pivots):
    row_ids = jnp.arange(R, dtype=jnp.int32)
    alive = (row_ids[None, :] < ranks[0][:, None])[:, :, None]
    current_samples = jnp.where(alive, samples, jnp.zeros_like(samples))
    current_omega = jnp.where(alive, omega, jnp.zeros_like(omega))
    coords = jnp.transpose(points, (1, 0, 2))
    stacked_ids = jnp.arange(2 * R, dtype=jnp.int32)
    for height in range(LEVELS):
        parents = current_samples.shape[0] // 2
        stride = 2 ** (height + 1)
        stacked_samples = current_samples.reshape(parents, 2 * R, NS)
        stacked_omega = current_omega.reshape(parents, 2 * R, NS)
        stacked_coords = coords.reshape(parents, 2, PDIM, R).transpose(0, 2, 1, 3).reshape(parents, PDIM, 2 * R)
        chosen = pivots[height, ::stride]
        parent_rank = ranks[height + 1, ::stride]

        def merge_node(inputs):
            node_samples, node_omega, node_coords, node_pivots, node_rank = inputs
            block = kernel_block(node_coords, node_coords, stacked_ids)
            reduced = (node_samples.astype(jnp.float32) - jnp.dot(block, node_omega, preferred_element_type=jnp.float32)).astype(jnp.bfloat16)
            living = (row_ids < node_rank)[:, None]
            new_samples = jnp.where(living, jnp.take(reduced, node_pivots, axis=0), jnp.zeros((R, NS), jnp.bfloat16))
            new_omega = jnp.where(living, jnp.take(node_omega, node_pivots, axis=0), jnp.zeros((R, NS), jnp.bfloat16))
            new_coords = jnp.take(node_coords, node_pivots, axis=1)
            return new_samples, new_omega, new_coords

        current_samples, current_omega, coords = lax.map(merge_node, (stacked_samples, stacked_omega, stacked_coords, chosen, parent_rank))
    return jnp.repeat(current_samples, 2 ** LEVELS, axis=0)
```

```python
import functools
import math

import jax
import jax.numpy as jnp
from jax import lax
from jax.experimental import pallas as pl
from jax.experimental.pallas import tpu as pltpu
from jax.sharding import PartitionSpec as P

MESH = pl.DeviceIdType.MESH
BF = jnp.bfloat16
F32 = jnp.float32
I32 = jnp.int32
kernel_rate = 0.6

WORKERS = [(0, 0, 0), (1, 0, 0), (0, 0, 1), (1, 0, 1), (0, 0, 2), (1, 0, 2), (0, 0, 3), (1, 0, 3)]
SEND_ORDER = list(range(8))
FAR_FIRST = sorted(range(32), key=lambda c: -(c // 8 * 10 + min(c // 2 % 4, 4 - c // 2 % 4) * 2 + c % 2))


def total(flags):
    return functools.reduce(lambda a, b: a + b, flags)


def kernel(
    samples, omega, points, ranks, pivots, out,
    pts_v, piv_v, rank_s, meta_out, meta_in, om_in, sa_in, pick, mat, lift, lift_in, part, part_in, blocks,
    local_sem, send_sem, recv_sem, pair_sem,
):
    leaf = lax.axis_index("leaf")
    grid = lax.axis_index("grid")
    core = grid % 2
    x = grid // 4
    y = (grid // 2) % 2
    z = leaf % 4
    base = leaf - z
    y_flip = (leaf // 16) % 2
    z_flip = 3 * ((leaf % 16) // 8)
    ny = (y + y_flip) % 2
    nz = z + (z_flip // 3) * (3 - 2 * z)
    chip = nz * 8 + x * 2 + ny

    def device(number):
        cx, cy, cz = number // 2 % 4, number % 2, number // 8
        at_z = cz + (z_flip // 3) * (3 - 2 * cz)
        at_y = (cy + y_flip) % 2
        return (base + at_z, cx * 4 + at_y * 2 + core)

    worker_chips = [wz * 8 + wx * 2 + wy for wx, wy, wz in WORKERS]
    mine = total([jnp.where(chip == c, i + 1, 0) for i, c in enumerate(worker_chips)])
    is_worker = mine > 0
    slot = jnp.maximum(mine - 1, 0)
    my_columns = pl.ds(pl.multiple_of(slot * 128, 128), 128)
    peer = (leaf, grid + 1 - 2 * core)

    loads = [
        pltpu.make_async_copy(points, pts_v, local_sem.at[0]),
        pltpu.make_async_copy(pivots, piv_v, local_sem.at[1]),
        pltpu.make_async_copy(ranks, rank_s, local_sem.at[2]),
    ]
    for load in loads:
        load.start()

    barrier = pltpu.get_barrier_semaphore()

    @pl.when(is_worker)
    def _():
        for number in FAR_FIRST:

            @pl.when(chip != number)
            def _():
                pl.semaphore_signal(barrier, inc=1, device_id=device(number), device_id_type=MESH)

        pl.semaphore_signal(barrier, inc=1, device_id=peer, device_id_type=MESH)
        own = [
            pltpu.make_async_copy(omega.at[0, :, my_columns], om_in.at[chip], recv_sem.at[1]),
            pltpu.make_async_copy(samples.at[0, :, my_columns], sa_in.at[chip], recv_sem.at[2]),
        ]
        for copy in own:
            copy.start()

    for load in loads:
        load.wait()

    first_rank = rank_s[0, leaf]
    kept_rank = rank_s[1, leaf]
    child = (z // 2) % 2
    first_pivots = piv_v[0]
    last_pivots = piv_v[1]
    row = lax.broadcasted_iota(I32, (32, 512), 0)
    lane = lax.broadcasted_iota(I32, (32, 512), 1)
    own_row = (z % 2) * 512 + grid * 32 + row
    place = jnp.sum(jnp.where(first_pivots == own_row, lane + 1, 0).astype(F32), axis=1, keepdims=True)
    target = jnp.where(place > 0.5, child.astype(F32) * 512.0 + place - 1.0, -1.0)
    final = (
        jnp.sum(jnp.where(last_pivots.astype(F32) == target, lane + 1, 0).astype(F32), axis=1, keepdims=True) - 1.0
    )
    column = lax.broadcasted_iota(I32, (32, 1), 0)
    alive = (grid * 32 + column < first_rank).astype(F32)
    kept = alive * ((place > 0.5) & (place < kept_rank.astype(F32) + 0.5)).astype(F32)
    side = child.astype(F32)
    high = jnp.floor((final + 1.0) * (1.0 / 32.0))
    low = final + 1.0 - 32.0 * high
    field = lax.broadcasted_iota(I32, (32, 128), 1)
    fields = jnp.where(field == 11, side, 0.0)
    fields = jnp.where(field == 12, alive * (1.0 - side) + kept, fields)
    fields = jnp.where(field == 13, alive * (2.0 * side - 1.0), fields)
    fields = jnp.where(field == 14, high, fields)
    fields = jnp.where(field == 15, low, fields)
    coords = pts_v[:, 0, :].astype(F32)
    norm = jnp.sum(coords * coords, axis=0, keepdims=True)
    norm_a = norm.astype(BF).astype(F32)
    norm_b = (norm - norm_a).astype(BF).astype(F32)
    norm_c = norm - norm_a - norm_b
    sub = lax.broadcasted_iota(I32, (8, 32), 0)
    norms = jnp.where(sub == 0, norm_a, jnp.where(sub == 1, norm_b, jnp.where(sub == 2, norm_c, 0.0)))
    upper = jnp.concatenate([coords, norms], axis=0).astype(BF)
    spot = (
        lax.broadcasted_iota(I32, (32, 128), 1) == lax.broadcasted_iota(I32, (32, 128), 0) + (chip % 4) * 32
    ).astype(BF)
    tile = jnp.dot(upper, spot, preferred_element_type=F32)
    lower = lax.dot_general(fields.astype(BF), spot, (((0,), (0,)), ((), ())), preferred_element_type=F32)
    meta_out[...] = (tile + lower[0:16]).astype(BF)

    @pl.when(is_worker)
    def _():
        copy = pltpu.make_async_copy(meta_out, meta_in.at[chip], recv_sem.at[0])
        copy.start()

    pl.semaphore_wait(barrier, 8)

    def send_all(source, target_ref, number):
        for w in SEND_ORDER:

            @pl.when(chip != worker_chips[w])
            def _():
                pltpu.make_async_remote_copy(
                    src_ref=source(w),
                    dst_ref=target_ref.at[chip],
                    send_sem=send_sem.at[number],
                    recv_sem=recv_sem.at[number],
                    device_id=device(worker_chips[w]),
                    device_id_type=MESH,
                ).start()

    send_all(lambda w: meta_out, meta_in, 0)
    send_all(lambda w: omega.at[0, :, pl.ds(128 * w, 128)], om_in, 1)
    send_all(lambda w: samples.at[0, :, pl.ds(128 * w, 128)], sa_in, 2)

    def await_bytes(ref, sem):
        pltpu.make_async_copy(ref, ref, sem).wait()

    @pl.when(is_worker)
    def _():
        await_bytes(meta_in, recv_sem.at[0])
        tiles = []
        for group in range(8):
            tiles.append(total([meta_in[4 * group + q].astype(F32) for q in range(4)]))
        meta = jnp.concatenate(tiles, axis=1)
        position = meta[14:15] * 32.0 + meta[15:16] - 1.0
        part_row = lax.broadcasted_iota(I32, (16, 1024), 0)
        right = jnp.where(part_row < 11, meta, jnp.where(part_row < 14, 1.0, 0.0)).astype(BF)
        shift = jnp.concatenate([meta[13:16], meta[0:13]], axis=0)
        raised = jnp.where(
            part_row < 8, -2.0 * meta, jnp.where((part_row >= 11) & (part_row < 14), shift, 0.0)
        )
        raised = jnp.where(part_row == 14, meta[11:12], raised).astype(BF)
        factor = jnp.where(part_row == 14, meta[13:14], jnp.where(part_row == 15, meta[12:13], 0.0)).astype(BF)

        for chunk in range(8):
            line = lax.broadcasted_iota(I32, (64, 1), 0) + 64 * chunk
            order = (line % 256) // 32 * 64 + line // 256 * 32 + line % 32
            hit = (position == order.astype(F32)).astype(BF)
            pick[pl.ds(64 * chunk, 64), :] = hit
        picked = lax.dot_general(pick[...], raised, (((1,), (1,)), ((), ())), preferred_element_type=F32)
        lift[:, 0:16] = picked.astype(BF)
        swap = pltpu.make_async_remote_copy(
            src_ref=lift, dst_ref=lift_in, send_sem=pair_sem.at[0], recv_sem=pair_sem.at[1],
            device_id=peer, device_id_type=MESH,
        )
        swap.start()
        swap.wait_recv()
        spread = lax.broadcasted_iota(I32, (512, 16), 1)
        ones = ((spread >= 8) & (spread < 11)) | (spread == 15)
        left = picked + lift_in[:, 0:16].astype(F32) + jnp.where(ones, 1.0, 0.0)
        left = left.astype(BF)
        scale = -kernel_rate * math.log2(math.e)
        for chunk in range(8):
            rows = slice(64 * chunk, 64 * chunk + 64)
            distance = jnp.dot(left[rows], right, preferred_element_type=F32)
            coef = jnp.dot(left[rows], factor, preferred_element_type=F32)
            diagonal = pick[rows, :].astype(F32)
            entry = (jnp.exp2(distance * scale) + diagonal).astype(BF)
            mat[rows, :] = entry * coef.astype(BF)

        await_bytes(om_in, recv_sem.at[1])
        product = jnp.dot(mat[...], om_in[...].reshape(1024, 128), preferred_element_type=F32)
        await_bytes(sa_in, recv_sem.at[2])
        chosen = jnp.dot(pick[...], sa_in[...].reshape(1024, 128), preferred_element_type=F32)
        part[...] = chosen - product
        trade = pltpu.make_async_remote_copy(
            src_ref=part.at[pl.ds(pl.multiple_of(256 * (1 - core), 256), 256)], dst_ref=part_in,
            send_sem=pair_sem.at[2], recv_sem=pair_sem.at[3], device_id=peer, device_id_type=MESH,
        )
        trade.start()
        trade.wait_recv()
        last_rank = rank_s[2, leaf]
        mine_rows = part[pl.ds(pl.multiple_of(256 * core, 256), 256)] + part_in[...]
        line = lax.broadcasted_iota(I32, (256, 128), 0)
        order = line // 32 * 64 + core * 32 + line % 32
        mine_rows = jnp.where(order < last_rank, mine_rows, 0.0).astype(BF)
        blocks[...] = mine_rows.reshape(8, 32, 128)

        for number in FAR_FIRST[::-1]:
            block = blocks.at[number // 2 % 4 * 2 + (number % 2 + y_flip) % 2]

            @pl.when(chip != number)
            def _():
                pltpu.make_async_remote_copy(
                    src_ref=block,
                    dst_ref=out.at[0, :, my_columns],
                    send_sem=send_sem.at[3],
                    recv_sem=recv_sem.at[3],
                    device_id=device(number),
                    device_id_type=MESH,
                ).start()

        pltpu.make_async_copy(blocks.at[x * 2 + y], out.at[0, :, my_columns], recv_sem.at[3]).start()

    await_bytes(out, recv_sem.at[3])

    @pl.when(is_worker)
    def _():
        swap = pltpu.make_async_copy(lift, lift_in, pair_sem.at[0])
        swap.wait()
        trade = pltpu.make_async_copy(part_in, part_in, pair_sem.at[2])
        trade.wait()
        await_bytes(om_in.at[pl.ds(0, 31)], send_sem.at[3])
        await_bytes(meta_in.at[pl.ds(0, 7)], send_sem.at[0])
        await_bytes(om_in.at[pl.ds(0, 7)], send_sem.at[1])
        await_bytes(sa_in.at[pl.ds(0, 7)], send_sem.at[2])

    @pl.when(jnp.logical_not(is_worker))
    def _():
        await_bytes(meta_in.at[pl.ds(0, 8)], send_sem.at[0])
        await_bytes(om_in.at[pl.ds(0, 8)], send_sem.at[1])
        await_bytes(sa_in.at[pl.ds(0, 8)], send_sem.at[2])


def body(samples, omega, points, ranks, pivots):
    anywhere = pl.BlockSpec(memory_space=pl.ANY)
    return pl.pallas_call(
        kernel,
        out_shape=jax.ShapeDtypeStruct((1, 32, 1024), BF),
        in_specs=[anywhere] * 5,
        out_specs=pl.BlockSpec(memory_space=pltpu.VMEM),
        scratch_shapes=[
            pltpu.VMEM((8, 1, 32), BF),
            pltpu.VMEM((2, 1, 512), I32),
            pltpu.SMEM((3, 32), I32),
            pltpu.VMEM((16, 128), BF),
            pltpu.VMEM((32, 16, 128), BF),
            pltpu.VMEM((32, 32, 128), BF),
            pltpu.VMEM((32, 32, 128), BF),
            pltpu.VMEM((512, 1024), BF),
            pltpu.VMEM((512, 1024), BF),
            pltpu.VMEM((512, 128), BF),
            pltpu.VMEM((512, 128), BF),
            pltpu.VMEM((512, 128), F32),
            pltpu.VMEM((256, 128), F32),
            pltpu.VMEM((8, 32, 128), BF),
            pltpu.SemaphoreType.DMA((3,)),
            pltpu.SemaphoreType.DMA((4,)),
            pltpu.SemaphoreType.DMA((4,)),
            pltpu.SemaphoreType.DMA((4,)),
        ],
        compiler_params=pltpu.CompilerParams(
            collective_id=0, has_side_effects=True, vmem_limit_bytes=40 * 2**20
        ),
        cost_estimate=pl.CostEstimate(flops=300_000_000, bytes_accessed=200_000, transcendentals=524288),
    )(samples, omega, points, ranks, pivots)


def solution(mesh):
    return jax.shard_map(
        body,
        mesh=mesh,
        in_specs=(
            P("leaf", "grid", None),
            P("leaf", "grid", None),
            P(None, "leaf", "grid"),
            P(),
            P(None, "leaf", None),
        ),
        out_specs=P("leaf", "grid", None),
        check_vma=False,
    )
```

```python
import functools
import math

import jax
import jax.numpy as jnp
from jax import lax
from jax.experimental import pallas as pl
from jax.experimental.pallas import tpu as pltpu
from jax.sharding import PartitionSpec as P

MESH = pl.DeviceIdType.MESH
BF = jnp.bfloat16
F32 = jnp.float32
I32 = jnp.int32
kernel_rate = 0.6

WORKERS = [(0,0,0),(1,0,1),(2,0,0),(3,0,1),(0,0,2),(1,1,0),(0,1,1),(3,1,0)]
SEND_ORDER = list(range(8))
FAR_FIRST = sorted(range(32), key=lambda c: -(c // 8 * 10 + min(c // 2 % 4, 4 - c // 2 % 4) * 2 + c % 2))


def total(flags):
    return functools.reduce(lambda a, b: a + b, flags)


def kernel(
    samples, omega, points, ranks, pivots, out,
    pts_v, piv_v, rank_s, meta_out, meta_in, om_in, sa_in, pick, mat, lift, lift_in, part, part_in, blocks,
    local_sem, send_sem, recv_sem, pair_sem,
):
    leaf = lax.axis_index("leaf")
    grid = lax.axis_index("grid")
    core = grid % 2
    x = grid // 4
    y = (grid // 2) % 2
    z = leaf % 4
    base = leaf - z
    y_flip = (leaf // 16) % 2
    z_flip = 3 * ((leaf % 16) // 8)
    ny = (y + y_flip) % 2
    nz = z + (z_flip // 3) * (3 - 2 * z)
    chip = nz * 8 + x * 2 + ny

    def device(number):
        cx, cy, cz = number // 2 % 4, number % 2, number // 8
        at_z = cz + (z_flip // 3) * (3 - 2 * cz)
        at_y = (cy + y_flip) % 2
        return (base + at_z, cx * 4 + at_y * 2 + core)

    worker_chips = [wz * 8 + wx * 2 + wy for wx, wy, wz in WORKERS]
    mine = total([jnp.where(chip == c, i + 1, 0) for i, c in enumerate(worker_chips)])
    is_worker = mine > 0
    slot = jnp.maximum(mine - 1, 0)
    my_columns = pl.ds(pl.multiple_of(slot * 128, 128), 128)
    peer = (leaf, grid + 1 - 2 * core)

    loads = [
        pltpu.make_async_copy(points, pts_v, local_sem.at[0]),
        pltpu.make_async_copy(pivots, piv_v, local_sem.at[1]),
        pltpu.make_async_copy(ranks, rank_s, local_sem.at[2]),
    ]
    for load in loads:
        load.start()

    barrier = pltpu.get_barrier_semaphore()

    @pl.when(is_worker)
    def _():
        for number in FAR_FIRST:

            @pl.when(chip != number)
            def _():
                pl.semaphore_signal(barrier, inc=1, device_id=device(number), device_id_type=MESH)

        pl.semaphore_signal(barrier, inc=1, device_id=peer, device_id_type=MESH)
        own = [
            pltpu.make_async_copy(omega.at[0, :, my_columns], om_in.at[chip], recv_sem.at[1]),
            pltpu.make_async_copy(samples.at[0, :, my_columns], sa_in.at[chip], recv_sem.at[2]),
        ]
        for copy in own:
            copy.start()

    for load in loads:
        load.wait()

    first_rank = rank_s[0, leaf]
    kept_rank = rank_s[1, leaf]
    child = (z // 2) % 2
    first_pivots = piv_v[0]
    last_pivots = piv_v[1]
    row = lax.broadcasted_iota(I32, (32, 512), 0)
    lane = lax.broadcasted_iota(I32, (32, 512), 1)
    own_row = (z % 2) * 512 + grid * 32 + row
    place = jnp.sum(jnp.where(first_pivots == own_row, lane + 1, 0).astype(F32), axis=1, keepdims=True)
    target = jnp.where(place > 0.5, child.astype(F32) * 512.0 + place - 1.0, -1.0)
    final = (
        jnp.sum(jnp.where(last_pivots.astype(F32) == target, lane + 1, 0).astype(F32), axis=1, keepdims=True) - 1.0
    )
    column = lax.broadcasted_iota(I32, (32, 1), 0)
    alive = (grid * 32 + column < first_rank).astype(F32)
    kept = alive * ((place > 0.5) & (place < kept_rank.astype(F32) + 0.5)).astype(F32)
    side = child.astype(F32)
    high = jnp.floor((final + 1.0) * (1.0 / 32.0))
    low = final + 1.0 - 32.0 * high
    field = lax.broadcasted_iota(I32, (32, 128), 1)
    fields = jnp.where(field == 11, side, 0.0)
    fields = jnp.where(field == 12, alive * (1.0 - side) + kept, fields)
    fields = jnp.where(field == 13, alive * (2.0 * side - 1.0), fields)
    fields = jnp.where(field == 14, high, fields)
    fields = jnp.where(field == 15, low, fields)
    coords = pts_v[...].astype(F32)
    norm = jnp.sum(coords * coords, axis=0, keepdims=True)
    norm_a = norm.astype(BF).astype(F32)
    norm_b = (norm - norm_a).astype(BF).astype(F32)
    norm_c = norm - norm_a - norm_b
    sub = lax.broadcasted_iota(I32, (8, 32), 0)
    norms = jnp.where(sub == 0, norm_a, jnp.where(sub == 1, norm_b, jnp.where(sub == 2, norm_c, 0.0)))
    upper = jnp.concatenate([coords, norms], axis=0).astype(BF)
    spot = (
        lax.broadcasted_iota(I32, (32, 128), 1) == lax.broadcasted_iota(I32, (32, 128), 0) + (chip % 4) * 32
    ).astype(BF)
    tile = jnp.dot(upper, spot, preferred_element_type=F32)
    lower = lax.dot_general(fields.astype(BF), spot, (((0,), (0,)), ((), ())), preferred_element_type=F32)
    meta_out[...] = (tile + lower[0:16]).astype(BF)

    @pl.when(is_worker)
    def _():
        copy = pltpu.make_async_copy(meta_out, meta_in.at[chip], recv_sem.at[0])
        copy.start()

    pl.semaphore_wait(barrier, 8)

    def send_all(source, target_ref, number):
        for w in SEND_ORDER:

            @pl.when(chip != worker_chips[w])
            def _():
                pltpu.make_async_remote_copy(
                    src_ref=source(w),
                    dst_ref=target_ref.at[chip],
                    send_sem=send_sem.at[number],
                    recv_sem=recv_sem.at[number],
                    device_id=device(worker_chips[w]),
                    device_id_type=MESH,
                ).start()

    send_all(lambda w: meta_out, meta_in, 0)
    send_all(lambda w: samples.at[0, :, pl.ds(128 * w, 128)], sa_in, 2)
    send_all(lambda w: omega.at[0, :, pl.ds(128 * w, 128)], om_in, 1)

    def await_bytes(ref, sem):
        pltpu.make_async_copy(ref, ref, sem).wait()

    @pl.when(is_worker)
    def _():
        await_bytes(meta_in, recv_sem.at[0])
        tiles = []
        for group in range(8):
            tiles.append(total([meta_in[4 * group + q].astype(F32) for q in range(4)]))
        meta = jnp.concatenate(tiles, axis=1)
        position = meta[14:15] * 32.0 + meta[15:16] - 1.0
        part_row = lax.broadcasted_iota(I32, (16, 1024), 0)
        right = jnp.where(part_row < 11, meta, jnp.where(part_row < 14, 1.0, 0.0)).astype(BF)
        shift = jnp.concatenate([meta[13:16], meta[0:13]], axis=0)
        raised = jnp.where(
            part_row < 8, -2.0 * meta, jnp.where((part_row >= 11) & (part_row < 14), shift, 0.0)
        )
        raised = jnp.where(part_row == 14, meta[11:12], raised).astype(BF)
        factor = jnp.where(part_row == 14, meta[13:14], jnp.where(part_row == 15, meta[12:13], 0.0)).astype(BF)

        for chunk in range(8):
            line = lax.broadcasted_iota(I32, (64, 1), 0) + 64 * (chunk % 4)
            half = 1 - core if chunk < 4 else core
            order = line // 32 * 64 + half * 32 + line % 32
            hit = (position == order.astype(F32)).astype(BF)
            pick[pl.ds(64 * chunk, 64), :] = hit
        picked = lax.dot_general(pick[...], raised, (((1,), (1,)), ((), ())), preferred_element_type=F32)
        lift[0:256, 0:16] = picked[256:512].astype(BF)
        lift[256:512, 0:16] = picked[0:256].astype(BF)
        swap = pltpu.make_async_remote_copy(
            src_ref=lift, dst_ref=lift_in, send_sem=pair_sem.at[0], recv_sem=pair_sem.at[1],
            device_id=peer, device_id_type=MESH,
        )
        swap.start()
        await_bytes(sa_in, recv_sem.at[2])
        part[...] = jnp.dot(pick[...], sa_in[...].reshape(1024, 128), preferred_element_type=F32)
        swap.wait_recv()
        spread = lax.broadcasted_iota(I32, (512, 16), 1)
        ones = ((spread >= 8) & (spread < 11)) | (spread == 15)
        left = picked + lift_in[:, 0:16].astype(F32) + jnp.where(ones, 1.0, 0.0)
        left = left.astype(BF)
        scale = -kernel_rate * math.log2(math.e)

        def form(chunk):
            rows = slice(64 * chunk, 64 * chunk + 64)
            distance = jnp.dot(left[rows], right, preferred_element_type=F32)
            coef = jnp.dot(left[rows], factor, preferred_element_type=F32)
            diagonal = pick[rows, :].astype(F32)
            entry = (jnp.exp2(distance * scale) + diagonal).astype(BF)
            mat[rows, :] = entry * coef.astype(BF)

        for chunk in range(4):
            form(chunk)
        await_bytes(om_in, recv_sem.at[1])
        part[0:256] -= jnp.dot(mat[0:256], om_in[...].reshape(1024, 128), preferred_element_type=F32)
        trade = pltpu.make_async_remote_copy(
            src_ref=part.at[pl.ds(0, 256)], dst_ref=part_in,
            send_sem=pair_sem.at[2], recv_sem=pair_sem.at[3], device_id=peer, device_id_type=MESH,
        )
        trade.start()
        for chunk in range(4, 8):
            form(chunk)
        part[256:512] -= jnp.dot(mat[256:512], om_in[...].reshape(1024, 128), preferred_element_type=F32)
        trade.wait_recv()
        last_rank = rank_s[2, leaf]
        mine_rows = part[256:512] + part_in[...]
        line = lax.broadcasted_iota(I32, (256, 128), 0)
        order = line // 32 * 64 + core * 32 + line % 32
        mine_rows = jnp.where(order < last_rank, mine_rows, 0.0).astype(BF)
        blocks[...] = mine_rows.reshape(8, 32, 128)

        for number in FAR_FIRST[::-1]:
            block = blocks.at[number // 2 % 4 * 2 + (number % 2 + y_flip) % 2]

            @pl.when(chip != number)
            def _():
                pltpu.make_async_remote_copy(
                    src_ref=block,
                    dst_ref=out.at[0, :, my_columns],
                    send_sem=send_sem.at[3],
                    recv_sem=recv_sem.at[3],
                    device_id=device(number),
                    device_id_type=MESH,
                ).start()

        pltpu.make_async_copy(blocks.at[x * 2 + y], out.at[0, :, my_columns], recv_sem.at[3]).start()

    await_bytes(out, recv_sem.at[3])

    @pl.when(is_worker)
    def _():
        swap = pltpu.make_async_copy(lift, lift_in, pair_sem.at[0])
        swap.wait()
        trade = pltpu.make_async_copy(part_in, part_in, pair_sem.at[2])
        trade.wait()
        await_bytes(om_in.at[pl.ds(0, 31)], send_sem.at[3])
        await_bytes(meta_in.at[pl.ds(0, 7)], send_sem.at[0])
        await_bytes(om_in.at[pl.ds(0, 7)], send_sem.at[1])
        await_bytes(sa_in.at[pl.ds(0, 7)], send_sem.at[2])

    @pl.when(jnp.logical_not(is_worker))
    def _():
        await_bytes(meta_in.at[pl.ds(0, 8)], send_sem.at[0])
        await_bytes(om_in.at[pl.ds(0, 8)], send_sem.at[1])
        await_bytes(sa_in.at[pl.ds(0, 8)], send_sem.at[2])


def body(samples, omega, points, ranks, pivots):
    anywhere = pl.BlockSpec(memory_space=pl.ANY)
    return pl.pallas_call(
        kernel,
        out_shape=pltpu.VMEM((1, 32, 1024), BF),
        in_specs=[anywhere] * 5,
        out_specs=pl.BlockSpec(memory_space=pltpu.VMEM),
        scratch_shapes=[
            pltpu.VMEM((8, 32), BF),
            pltpu.VMEM((2, 1, 512), I32),
            pltpu.SMEM((3, 32), I32),
            pltpu.VMEM((16, 128), BF),
            pltpu.VMEM((32, 16, 128), BF),
            pltpu.VMEM((32, 32, 128), BF),
            pltpu.VMEM((32, 32, 128), BF),
            pltpu.VMEM((512, 1024), BF),
            pltpu.VMEM((512, 1024), BF),
            pltpu.VMEM((512, 128), BF),
            pltpu.VMEM((512, 128), BF),
            pltpu.VMEM((512, 128), F32),
            pltpu.VMEM((256, 128), F32),
            pltpu.VMEM((8, 32, 128), BF),
            pltpu.SemaphoreType.DMA((3,)),
            pltpu.SemaphoreType.DMA((4,)),
            pltpu.SemaphoreType.DMA((4,)),
            pltpu.SemaphoreType.DMA((4,)),
        ],
        compiler_params=pltpu.CompilerParams(
            collective_id=0, has_side_effects=True, vmem_limit_bytes=60 * 2**20
        ),
        cost_estimate=pl.CostEstimate(flops=300_000_000, bytes_accessed=200_000, transcendentals=524288),
    )(samples, omega, points[:, 0, :], ranks, pivots)


def solution(mesh):
    return jax.shard_map(
        body,
        mesh=mesh,
        in_specs=(
            P("leaf", "grid", None),
            P("leaf", "grid", None),
            P(None, "leaf", "grid"),
            P(),
            P(None, "leaf", None),
        ),
        out_specs=P("leaf", "grid", None),
        check_vma=False,
    )
```

```python
import functools
import math

import jax
import jax.numpy as jnp
from jax import lax
from jax.experimental import pallas as pl
from jax.experimental.pallas import tpu as pltpu
from jax.sharding import PartitionSpec as P

MESH = pl.DeviceIdType.MESH
BF = jnp.bfloat16
F32 = jnp.float32
I32 = jnp.int32
kernel_rate = 0.6

NEAR = [z * 8 + x * 2 + y for y, z in [(0, 0), (0, 1), (0, 2), (1, 0)] for x in (0, 1, 3, 2)]
MIDDLE = [p * 8 + c for p in (0, 1) for c in range(8)]
PLANES = [1, 2, 0, 3]
FAR_FIRST = sorted(range(32), key=lambda c: -(c // 8 * 10 + min(c // 2 % 4, 4 - c // 2 % 4) * 2 + c % 2))
OUT_ORDER = [p * 8 + c for c in [0, 2, 6, 1, 4, 3, 7, 5] for p in [0, 3, 2, 1]]


def total(flags):
    return functools.reduce(lambda a, b: a + b, flags)


def kernel(
    samples, omega, points, ranks, pivots, out,
    pts_v, piv_v, rank_s, om_v, sa_v, packed, meta_out, meta_in, meta_turn, data_in, pick, mat, lift, lift_in, part, part_in,
    blocks, pieces,
    local_sem, send_sem, recv_sem, pair_sem,
):
    leaf = lax.axis_index("leaf")
    grid = lax.axis_index("grid")
    core = grid % 2
    x = grid // 4
    y = (grid // 2) % 2
    z = leaf % 4
    base = leaf - z
    back = (leaf % 16) // 8
    plane = total([jnp.where(z == k + back * (PLANES[k] - k), k, 0) for k in range(4)])
    chip = plane * 8 + x * 2 + y

    def device(number):
        cx, cy, cz = number // 2 % 4, number % 2, number // 8
        return (base + cz + back * (PLANES[cz] - cz), cx * 4 + cy * 2 + core)

    def worker(w):
        a, b = NEAR[w], MIDDLE[w]
        plane_a, plane_b = a // 8, PLANES[b // 8]
        return (base + plane_a + back * (plane_b - plane_a), (a % 8 + back * (b % 8 - a % 8)) * 2 + core)

    worker_chips = [a + back * (b - a) for a, b in zip(NEAR, MIDDLE, strict=True)]
    mine = total([jnp.where(chip == c, i + 1, 0) for i, c in enumerate(worker_chips)])
    is_worker = mine > 0
    slot = jnp.maximum(mine - 1, 0)
    meta_slot = chip % 4 * 8 + chip // 4
    peer = (leaf, grid + 1 - 2 * core)

    loads = [
        pltpu.make_async_copy(omega.at[0], om_v, local_sem.at[3]),
        pltpu.make_async_copy(samples.at[0], sa_v, local_sem.at[4]),
        pltpu.make_async_copy(points, pts_v, local_sem.at[0]),
        pltpu.make_async_copy(pivots, piv_v, local_sem.at[1]),
        pltpu.make_async_copy(ranks, rank_s, local_sem.at[2]),
    ]
    for load in loads:
        load.start()

    barrier = pltpu.get_barrier_semaphore()

    @pl.when(is_worker)
    def _():
        for number in FAR_FIRST:

            @pl.when(chip != number)
            def _():
                pl.semaphore_signal(barrier, inc=1, device_id=device(number), device_id_type=MESH)

        pl.semaphore_signal(barrier, inc=1, device_id=peer, device_id_type=MESH)

    for load in loads:
        load.wait()

    first_rank = rank_s[0, leaf]
    kept_rank = rank_s[1, leaf]
    child = (z // 2) % 2
    first_pivots = piv_v[0]
    last_pivots = piv_v[1]
    row = lax.broadcasted_iota(I32, (32, 512), 0)
    lane = lax.broadcasted_iota(I32, (32, 512), 1)
    own_row = (z % 2) * 512 + grid * 32 + row
    place = jnp.sum(jnp.where(first_pivots == own_row, lane + 1, 0).astype(F32), axis=1, keepdims=True)
    target = jnp.where(place > 0.5, child.astype(F32) * 512.0 + place - 1.0, -1.0)
    final = (
        jnp.sum(jnp.where(last_pivots.astype(F32) == target, lane + 1, 0).astype(F32), axis=1, keepdims=True) - 1.0
    )
    column = lax.broadcasted_iota(I32, (32, 1), 0)
    alive = (grid * 32 + column < first_rank).astype(F32)
    kept = alive * ((place > 0.5) & (place < kept_rank.astype(F32) + 0.5)).astype(F32)
    side = child.astype(F32)
    high = jnp.floor((final + 1.0) * (1.0 / 32.0))
    low = final + 1.0 - 32.0 * high
    field = lax.broadcasted_iota(I32, (32, 128), 1)
    fields = jnp.where(field == 11, side, 0.0)
    fields = jnp.where(field == 12, alive * (1.0 - side) + kept, fields)
    fields = jnp.where(field == 13, alive * (2.0 * side - 1.0), fields)
    fields = jnp.where(field == 14, high, fields)
    fields = jnp.where(field == 15, low, fields)
    coords = pts_v[...].astype(F32)
    norm = jnp.sum(coords * coords, axis=0, keepdims=True)
    norm_a = norm.astype(BF).astype(F32)
    norm_b = (norm - norm_a).astype(BF).astype(F32)
    norm_c = norm - norm_a - norm_b
    sub = lax.broadcasted_iota(I32, (8, 32), 0)
    norms = jnp.where(sub == 0, norm_a, jnp.where(sub == 1, norm_b, jnp.where(sub == 2, norm_c, 0.0)))
    upper = jnp.concatenate([coords, norms], axis=0).astype(BF)
    repeat = (
        lax.broadcasted_iota(I32, (32, 128), 1) % 32 == lax.broadcasted_iota(I32, (32, 128), 0)
    ).astype(BF)
    tile = jnp.dot(upper, repeat, preferred_element_type=F32)
    lower = lax.dot_general(fields.astype(BF), repeat, (((0,), (0,)), ((), ())), preferred_element_type=F32)
    tile = tile + lower[0:16]
    at_field = lax.broadcasted_iota(I32, (16, 128), 0)
    at_block = lax.broadcasted_iota(I32, (16, 128), 1) // 32
    for part_of in range(4):
        chosen_row = jnp.where(at_field == 4 * part_of + at_block, tile, 0.0)
        meta_out[:, 128 * part_of : 128 * part_of + 128] = jnp.sum(chosen_row, axis=0, keepdims=True)

    left_half = lax.broadcasted_iota(I32, (32, 128), 1) < 64
    for v in range(8):
        o = om_v[:, 128 * v : 128 * v + 128].astype(F32)
        a = sa_v[:, 128 * v : 128 * v + 128].astype(F32)
        packed[2 * v] = jnp.where(left_half, o, pltpu.roll(a, 64, 1)).astype(BF)
        packed[2 * v + 1] = jnp.where(left_half, pltpu.roll(o, 64, 1), a).astype(BF)

    @pl.when(is_worker)
    def _():
        pltpu.make_async_copy(meta_out, meta_in.at[meta_slot], recv_sem.at[0]).start()
        pltpu.make_async_copy(packed.at[slot], data_in.at[chip], recv_sem.at[1]).start()

    pl.semaphore_wait(barrier, 16)

    def send_all(source, target, number):
        for w in range(16):

            @pl.when(chip != worker_chips[w])
            def _():
                pltpu.make_async_remote_copy(
                    src_ref=source(w),
                    dst_ref=target,
                    send_sem=send_sem.at[number],
                    recv_sem=recv_sem.at[number],
                    device_id=worker(w),
                    device_id_type=MESH,
                ).start()

    send_all(lambda w: meta_out, meta_in.at[meta_slot], 0)
    send_all(lambda w: packed.at[w], data_in.at[chip], 1)

    def await_bytes(ref, sem):
        pltpu.make_async_copy(ref, ref, sem).wait()

    @pl.when(is_worker)
    def _():
        await_bytes(meta_in, recv_sem.at[0])
        block = lax.broadcasted_iota(I32, (8, 128), 1) // 32
        for f in range(16):
            turned = jnp.zeros((8, 128), F32)
            for q in range(4):
                source = meta_in[8 * q : 8 * q + 8, 0, f // 4 * 128 : f // 4 * 128 + 128]
                shift_by = (q - f % 4) % 4 * 32
                turned = jnp.where(block == q, pltpu.roll(source, shift_by, 1) if shift_by else source, turned)
            meta_turn[f] = turned
        meta = jnp.concatenate([meta_turn[:, group, :] for group in range(8)], axis=1)
        position = meta[14:15] * 32.0 + meta[15:16] - 1.0
        part_row = lax.broadcasted_iota(I32, (16, 1024), 0)
        right = jnp.where(part_row < 11, meta, jnp.where(part_row < 14, 1.0, 0.0)).astype(BF)
        shift = jnp.concatenate([meta[13:16], meta[0:13]], axis=0)
        raised = jnp.where(
            part_row < 8, -2.0 * meta, jnp.where((part_row >= 11) & (part_row < 14), shift, 0.0)
        )
        raised = jnp.where(part_row == 14, meta[11:12], raised).astype(BF)
        factor = jnp.where(part_row == 14, meta[13:14], jnp.where(part_row == 15, meta[12:13], 0.0)).astype(BF)

        for chunk in range(8):
            line = lax.broadcasted_iota(I32, (64, 1), 0) + 64 * (chunk % 4)
            half = 1 - core if chunk < 4 else core
            order = line // 32 * 64 + half * 32 + line % 32
            hit = (position == order.astype(F32)).astype(BF)
            pick[pl.ds(64 * chunk, 64), :] = hit
        picked = lax.dot_general(pick[...], raised, (((1,), (1,)), ((), ())), preferred_element_type=F32)
        lift[0:256, 0:16] = picked[256:512].astype(BF)
        lift[256:512, 0:16] = picked[0:256].astype(BF)
        swap = pltpu.make_async_remote_copy(
            src_ref=lift, dst_ref=lift_in, send_sem=pair_sem.at[0], recv_sem=pair_sem.at[1],
            device_id=peer, device_id_type=MESH,
        )
        swap.start()
        swap.wait_recv()
        spread = lax.broadcasted_iota(I32, (512, 16), 1)
        ones = ((spread >= 8) & (spread < 11)) | (spread == 15)
        left = picked + lift_in[:, 0:16].astype(F32) + jnp.where(ones, 1.0, 0.0)
        left = left.astype(BF)
        scale = -kernel_rate * math.log2(math.e)

        def form(chunk):
            rows = slice(64 * chunk, 64 * chunk + 64)
            distance = jnp.dot(left[rows], right, preferred_element_type=F32)
            coef = jnp.dot(left[rows], factor, preferred_element_type=F32)
            diagonal = pick[rows, :].astype(F32)
            entry = (jnp.exp2(distance * scale) + diagonal).astype(BF)
            mat[rows, :] = entry * coef.astype(BF)

        left_lanes = lax.broadcasted_iota(I32, (8, 16, 128), 2) < 64

        def combine(first):
            rows = slice(first, first + 256)
            data = data_in[...].reshape(1024, 128)
            chosen = jnp.dot(pick[rows], data, preferred_element_type=F32).reshape(8, 32, 128)
            product = jnp.dot(mat[rows], data, preferred_element_type=F32).reshape(8, 32, 128)
            above = pltpu.roll(chosen[:, 0:16], 64, 2) - product[:, 0:16]
            below = chosen[:, 16:32] - pltpu.roll(product[:, 16:32], 64, 2)
            return jnp.where(left_lanes, above, below)

        for chunk in range(4):
            form(chunk)
        await_bytes(data_in, recv_sem.at[1])
        part[...] = combine(0)
        trade = pltpu.make_async_remote_copy(
            src_ref=part, dst_ref=part_in,
            send_sem=pair_sem.at[2], recv_sem=pair_sem.at[3], device_id=peer, device_id_type=MESH,
        )
        trade.start()
        for chunk in range(4, 8):
            form(chunk)
        mine_rows = combine(256)
        trade.wait_recv()
        last_rank = rank_s[2, leaf]
        mine_rows = mine_rows + part_in[...]
        order = (
            lax.broadcasted_iota(I32, (8, 16, 128), 0) * 64 + core * 32
            + jnp.where(left_lanes, 0, 16) + lax.broadcasted_iota(I32, (8, 16, 128), 1)
        )
        blocks[...] = jnp.where(order < last_rank, mine_rows, 0.0).astype(BF)

        for number in OUT_ORDER:
            block = blocks.at[number // 2 % 4 * 2 + number % 2]

            @pl.when(chip != number)
            def _():
                pltpu.make_async_remote_copy(
                    src_ref=block,
                    dst_ref=pieces.at[slot],
                    send_sem=send_sem.at[2],
                    recv_sem=recv_sem.at[2],
                    device_id=device(number),
                    device_id_type=MESH,
                ).start()

        pltpu.make_async_copy(blocks.at[x * 2 + y], pieces.at[slot], recv_sem.at[2]).start()

    await_bytes(pieces, recv_sem.at[2])
    left_part = lax.broadcasted_iota(I32, (16, 128), 1) < 64
    for v in range(8):
        even = pieces[2 * v].astype(F32)
        odd = pieces[2 * v + 1].astype(F32)
        columns = slice(128 * v, 128 * v + 128)
        out[0, 0:16, columns] = jnp.where(left_part, even, pltpu.roll(odd, 64, 1)).astype(BF)
        out[0, 16:32, columns] = jnp.where(left_part, pltpu.roll(even, 64, 1), odd).astype(BF)

    @pl.when(is_worker)
    def _():
        pltpu.make_async_copy(lift, lift_in, pair_sem.at[0]).wait()
        pltpu.make_async_copy(part, part_in, pair_sem.at[2]).wait()
        await_bytes(data_in.at[pl.ds(0, 31), pl.ds(0, 16)], send_sem.at[2])
        await_bytes(meta_in.at[pl.ds(0, 15)], send_sem.at[0])
        await_bytes(data_in.at[pl.ds(0, 15)], send_sem.at[1])

    @pl.when(jnp.logical_not(is_worker))
    def _():
        await_bytes(meta_in.at[pl.ds(0, 16)], send_sem.at[0])
        await_bytes(data_in.at[pl.ds(0, 16)], send_sem.at[1])


def body(samples, omega, points, ranks, pivots):
    anywhere = pl.BlockSpec(memory_space=pl.ANY)
    return pl.pallas_call(
        kernel,
        out_shape=pltpu.VMEM((1, 32, 1024), BF),
        in_specs=[anywhere] * 5,
        out_specs=pl.BlockSpec(memory_space=pltpu.VMEM),
        scratch_shapes=[
            pltpu.VMEM((8, 32), BF),
            pltpu.VMEM((2, 1, 512), I32),
            pltpu.SMEM((3, 32), I32),
            pltpu.VMEM((32, 1024), BF),
            pltpu.VMEM((32, 1024), BF),
            pltpu.VMEM((16, 32, 128), BF),
            pltpu.VMEM((1, 512), F32),
            pltpu.VMEM((32, 1, 512), F32),
            pltpu.VMEM((16, 8, 128), F32),
            pltpu.VMEM((32, 32, 128), BF),
            pltpu.VMEM((512, 1024), BF),
            pltpu.VMEM((512, 1024), BF),
            pltpu.VMEM((512, 128), BF),
            pltpu.VMEM((512, 128), BF),
            pltpu.VMEM((8, 16, 128), F32),
            pltpu.VMEM((8, 16, 128), F32),
            pltpu.VMEM((8, 16, 128), BF),
            pltpu.VMEM((16, 16, 128), BF),
            pltpu.SemaphoreType.DMA((5,)),
            pltpu.SemaphoreType.DMA((3,)),
            pltpu.SemaphoreType.DMA((3,)),
            pltpu.SemaphoreType.DMA((4,)),
        ],
        compiler_params=pltpu.CompilerParams(
            collective_id=0, has_side_effects=True, vmem_limit_bytes=60 * 2**20
        ),
        cost_estimate=pl.CostEstimate(flops=300_000_000, bytes_accessed=200_000, transcendentals=524288),
    )(samples, omega, points[:, 0, :], ranks, pivots)


def solution(mesh):
    return jax.shard_map(
        body,
        mesh=mesh,
        in_specs=(
            P("leaf", "grid", None),
            P("leaf", "grid", None),
            P(None, "leaf", "grid"),
            P(),
            P(None, "leaf", None),
        ),
        out_specs=P("leaf", "grid", None),
        check_vma=False,
    )
```

```python
import functools
import math

import jax
import jax.numpy as jnp
from jax import lax
from jax.experimental import pallas as pl
from jax.experimental.pallas import tpu as pltpu
from jax.sharding import PartitionSpec as P

MESH = pl.DeviceIdType.MESH
BF = jnp.bfloat16
F32 = jnp.float32
I32 = jnp.int32
kernel_rate = 0.6

NEAR = [3, 7, 4, 2, 1, 6, 10, 14, 9, 13, 8, 16, 19, 22, 20, 17]
MIDDLE = [p * 8 + c for p in (0, 3) for c in range(8)]
PLANES = [1, 3, 0, 2]
FAR_FIRST = sorted(range(32), key=lambda c: -(c // 8 * 10 + min(c // 2 % 4, 4 - c // 2 % 4) * 2 + c % 2))
OUT_ORDER = [[p * 8 + c for p in range(4) for c in cs] for cs in ((0, 2, 1, 3), (6, 4, 7, 5))]


def total(flags):
    return functools.reduce(lambda a, b: a + b, flags)


def kernel(
    samples, omega, points, ranks, pivots, out,
    pts_v, piv_v, rank_s, om_v, sa_v, packed, meta_out, meta_in, meta_turn, data_in, pick, mat, lift, lift_in, part, part_in,
    blocks, pieces,
    local_sem, send_sem, recv_sem, pair_sem,
):
    leaf = lax.axis_index("leaf")
    grid = lax.axis_index("grid")
    core = grid % 2
    x = grid // 4
    y = (grid // 2) % 2
    z = leaf % 4
    base = leaf - z
    back = (leaf % 16) // 8
    plane = total([jnp.where(z == k + back * (PLANES[k] - k), k, 0) for k in range(4)])
    chip = plane * 8 + x * 2 + y

    def device(number):
        cx, cy, cz = number // 2 % 4, number % 2, number // 8
        return (base + cz + back * (PLANES[cz] - cz), cx * 4 + cy * 2 + core)

    def worker(w):
        a, b = NEAR[w], MIDDLE[w]
        plane_a, plane_b = a // 8, PLANES[b // 8]
        return (base + plane_a + back * (plane_b - plane_a), (a % 8 + back * (b % 8 - a % 8)) * 2 + core)

    worker_chips = [a + back * (b - a) for a, b in zip(NEAR, MIDDLE, strict=True)]
    mine = total([jnp.where(chip == c, i + 1, 0) for i, c in enumerate(worker_chips)])
    is_worker = mine > 0
    slot = jnp.maximum(mine - 1, 0)
    meta_slot = chip % 4 * 8 + chip // 4
    peer = (leaf, grid + 1 - 2 * core)

    loads = [
        pltpu.make_async_copy(points, pts_v, local_sem.at[0]),
        pltpu.make_async_copy(pivots, piv_v, local_sem.at[1]),
        pltpu.make_async_copy(ranks, rank_s, local_sem.at[2]),
    ]
    bulk = [
        pltpu.make_async_copy(omega.at[0], om_v, local_sem.at[3]),
        pltpu.make_async_copy(samples.at[0], sa_v, local_sem.at[4]),
    ]
    for load in loads + bulk:
        load.start()

    barrier = pltpu.get_barrier_semaphore()

    @pl.when(is_worker)
    def _():
        for number in FAR_FIRST[::-1]:

            @pl.when(chip != number)
            def _():
                pl.semaphore_signal(barrier, inc=1, device_id=device(number), device_id_type=MESH)

        pl.semaphore_signal(barrier, inc=1, device_id=peer, device_id_type=MESH)

    for load in loads:
        load.wait()

    first_rank = rank_s[0, leaf]
    kept_rank = rank_s[1, leaf]
    child = (z // 2) % 2
    first_pivots = piv_v[0]
    last_pivots = piv_v[1]
    row = lax.broadcasted_iota(I32, (32, 512), 0)
    lane = lax.broadcasted_iota(I32, (32, 512), 1)
    own_row = (z % 2) * 512 + grid * 32 + row
    place = jnp.sum(jnp.where(first_pivots == own_row, lane + 1, 0).astype(F32), axis=1, keepdims=True)
    target = jnp.where(place > 0.5, child.astype(F32) * 512.0 + place - 1.0, -1.0)
    final = (
        jnp.sum(jnp.where(last_pivots.astype(F32) == target, lane + 1, 0).astype(F32), axis=1, keepdims=True) - 1.0
    )
    column = lax.broadcasted_iota(I32, (32, 1), 0)
    alive = (grid * 32 + column < first_rank).astype(F32)
    kept = alive * ((place > 0.5) & (place < kept_rank.astype(F32) + 0.5)).astype(F32)
    side = child.astype(F32)
    high = jnp.floor((final + 1.0) * (1.0 / 32.0))
    low = final + 1.0 - 32.0 * high
    field = lax.broadcasted_iota(I32, (32, 128), 1)
    fields = jnp.where(field == 11, side, 0.0)
    fields = jnp.where(field == 12, alive * (1.0 - side) + kept, fields)
    fields = jnp.where(field == 13, alive * (2.0 * side - 1.0), fields)
    fields = jnp.where(field == 14, high, fields)
    fields = jnp.where(field == 15, low, fields)
    coords = pts_v[...].astype(F32)
    norm = jnp.sum(coords * coords, axis=0, keepdims=True)
    norm_a = norm.astype(BF).astype(F32)
    norm_b = (norm - norm_a).astype(BF).astype(F32)
    norm_c = norm - norm_a - norm_b
    sub = lax.broadcasted_iota(I32, (8, 32), 0)
    norms = jnp.where(sub == 0, norm_a, jnp.where(sub == 1, norm_b, jnp.where(sub == 2, norm_c, 0.0)))
    upper = jnp.concatenate([coords, norms], axis=0).astype(BF)
    repeat = (
        lax.broadcasted_iota(I32, (32, 128), 1) % 32 == lax.broadcasted_iota(I32, (32, 128), 0)
    ).astype(BF)
    tile = jnp.dot(upper, repeat, preferred_element_type=F32)
    lower = lax.dot_general(fields.astype(BF), repeat, (((0,), (0,)), ((), ())), preferred_element_type=F32)
    tile = tile + lower[0:16]
    at_field = lax.broadcasted_iota(I32, (16, 128), 0)
    at_block = lax.broadcasted_iota(I32, (16, 128), 1) // 32
    for part_of in range(4):
        chosen_row = jnp.where(at_field == 4 * part_of + (at_block + 4 - chip % 4) % 4, tile, 0.0)
        meta_out[:, 128 * part_of : 128 * part_of + 128] = jnp.sum(chosen_row, axis=0, keepdims=True)

    @pl.when(is_worker)
    def _():
        pltpu.make_async_copy(meta_out, meta_in.at[meta_slot], recv_sem.at[0]).start()

    pl.semaphore_wait(barrier, 16)

    def send_all(source, target, number):
        for w in range(16):

            @pl.when(chip != worker_chips[w])
            def _():
                pltpu.make_async_remote_copy(
                    src_ref=source(w),
                    dst_ref=target,
                    send_sem=send_sem.at[number],
                    recv_sem=recv_sem.at[number],
                    device_id=worker(w),
                    device_id_type=MESH,
                ).start()

    send_all(lambda w: meta_out, meta_in.at[meta_slot], 0)
    for load in bulk:
        load.wait()

    left_half = lax.broadcasted_iota(I32, (32, 128), 1) < 64
    for v in range(8):
        o = om_v[:, 128 * v : 128 * v + 128].astype(F32)
        a = sa_v[:, 128 * v : 128 * v + 128].astype(F32)
        packed[2 * v] = jnp.where(left_half, o, pltpu.roll(a, 64, 1)).astype(BF)
        packed[2 * v + 1] = jnp.where(left_half, pltpu.roll(o, 64, 1), a).astype(BF)

    @pl.when(is_worker)
    def _():
        pltpu.make_async_copy(packed.at[slot], data_in.at[chip], recv_sem.at[1]).start()

    send_all(lambda w: packed.at[w], data_in.at[chip], 1)

    def await_bytes(ref, sem):
        pltpu.make_async_copy(ref, ref, sem).wait()

    @pl.when(is_worker)
    def _():
        await_bytes(meta_in, recv_sem.at[0])
        block = lax.broadcasted_iota(I32, (8, 128), 1) // 32
        for f in range(16):
            turned = meta_in[0:8, 0, f // 4 * 128 : f // 4 * 128 + 128]
            for q in range(1, 4):
                source = meta_in[8 * q : 8 * q + 8, 0, f // 4 * 128 : f // 4 * 128 + 128]
                turned = jnp.where(block == (q + f % 4) % 4, source, turned)
            turned = pltpu.roll(turned, (4 - f % 4) * 32, 1) if f % 4 else turned
            meta_turn[f] = turned
        meta = jnp.concatenate([meta_turn[:, group, :] for group in range(8)], axis=1)
        position = meta[14:15] * 32.0 + meta[15:16] - 1.0
        part_row = lax.broadcasted_iota(I32, (16, 1024), 0)
        right = jnp.where(part_row < 11, meta, jnp.where(part_row < 14, 1.0, 0.0)).astype(BF)
        shift = jnp.concatenate([meta[13:16], meta[0:13]], axis=0)
        raised = jnp.where(
            part_row < 8, -2.0 * meta, jnp.where((part_row >= 11) & (part_row < 14), shift, 0.0)
        )
        raised = jnp.where(part_row == 14, meta[11:12], raised).astype(BF)
        factor = jnp.where(part_row == 14, meta[13:14], jnp.where(part_row == 15, meta[12:13], 0.0)).astype(BF)

        for chunk in range(8):
            line = lax.broadcasted_iota(I32, (64, 1), 0) + 64 * (chunk % 4)
            half = 1 - core if chunk < 4 else core
            order = line // 32 * 64 + half * 32 + line % 32
            hit = (position == order.astype(F32)).astype(BF)
            pick[pl.ds(64 * chunk, 64), :] = hit
        eight = jnp.concatenate([raised] * 8, axis=0)
        picked = lax.dot_general(pick[...], eight, (((1,), (1,)), ((), ())), preferred_element_type=F32)
        chunk_lane = lax.broadcasted_iota(I32, (64, 128), 1) // 16
        gathered = total([jnp.where(chunk_lane == g, picked[64 * g : 64 * g + 64], 0.0) for g in range(8)])
        lift[...] = pltpu.roll(gathered, 64, 1).astype(BF)
        swap = pltpu.make_async_remote_copy(
            src_ref=lift, dst_ref=lift_in, send_sem=pair_sem.at[0], recv_sem=pair_sem.at[1],
            device_id=peer, device_id_type=MESH,
        )
        swap.start()
        right = jnp.concatenate([right] * 8, axis=0)
        factor = jnp.concatenate([factor] * 8, axis=0)
        swap.wait_recv()
        spread = lax.broadcasted_iota(I32, (64, 128), 1) % 16
        ones = ((spread >= 8) & (spread < 11)) | (spread == 15)
        left = gathered + lift_in[...].astype(F32) + jnp.where(ones, 1.0, 0.0)
        scale = -kernel_rate * math.log2(math.e)

        def form(chunk):
            rows = slice(64 * chunk, 64 * chunk + 64)
            one = jnp.where(chunk_lane == chunk, left, 0.0).astype(BF)
            distance = jnp.dot(one, right, preferred_element_type=F32)
            coef = jnp.dot(one, factor, preferred_element_type=F32)
            diagonal = pick[rows, :].astype(F32)
            entry = (jnp.exp2(distance * scale) + diagonal).astype(BF)
            mat[rows, :] = entry * coef.astype(BF)

        left_lanes = lax.broadcasted_iota(I32, (8, 16, 128), 2) < 64

        def combine(first, count):
            rows = slice(first, first + 32 * count)
            data = data_in[...].reshape(1024, 128)
            chosen = jnp.dot(pick[rows], data, preferred_element_type=F32).reshape(count, 32, 128)
            product = jnp.dot(mat[rows], data, preferred_element_type=F32).reshape(count, 32, 128)
            above = pltpu.roll(chosen[:, 0:16], 64, 2) - product[:, 0:16]
            below = chosen[:, 16:32] - pltpu.roll(product[:, 16:32], 64, 2)
            return jnp.where(left_lanes[0:count], above, below)

        for chunk in range(4):
            form(chunk)
        await_bytes(data_in, recv_sem.at[1])
        trades = []
        for k in range(2):
            part[4 * k : 4 * k + 4] = combine(128 * k, 4)
            trade = pltpu.make_async_remote_copy(
                src_ref=part.at[pl.ds(4 * k, 4)], dst_ref=part_in.at[pl.ds(4 * k, 4)],
                send_sem=pair_sem.at[2 + 2 * k], recv_sem=pair_sem.at[3 + 2 * k],
                device_id=peer, device_id_type=MESH,
            )
            trade.start()
            trades.append(trade)
        for chunk in range(4, 8):
            form(chunk)
        mine_rows = combine(256, 8)
        last_rank = rank_s[2, leaf]
        order = (
            lax.broadcasted_iota(I32, (8, 16, 128), 0) * 64 + core * 32
            + jnp.where(left_lanes, 0, 16) + lax.broadcasted_iota(I32, (8, 16, 128), 1)
        )
        for k in range(2):
            trades[k].wait_recv()
            these = slice(4 * k, 4 * k + 4)
            blocks[these] = jnp.where(order[these] < last_rank, mine_rows[these] + part_in[these], 0.0).astype(BF)
            for number in OUT_ORDER[k]:
                block = blocks.at[number % 8]

                @pl.when(chip != number)
                def _():
                    pltpu.make_async_remote_copy(
                        src_ref=block,
                        dst_ref=pieces.at[slot],
                        send_sem=send_sem.at[2],
                        recv_sem=recv_sem.at[2],
                        device_id=device(number),
                        device_id_type=MESH,
                    ).start()

        pltpu.make_async_copy(blocks.at[x * 2 + y], pieces.at[slot], recv_sem.at[2]).start()

    await_bytes(pieces, recv_sem.at[2])
    left_part = lax.broadcasted_iota(I32, (16, 128), 1) < 64
    for v in range(8):
        even = pieces[2 * v].astype(F32)
        odd = pieces[2 * v + 1].astype(F32)
        columns = slice(128 * v, 128 * v + 128)
        out[0, 0:16, columns] = jnp.where(left_part, even, pltpu.roll(odd, 64, 1)).astype(BF)
        out[0, 16:32, columns] = jnp.where(left_part, pltpu.roll(even, 64, 1), odd).astype(BF)

    @pl.when(is_worker)
    def _():
        pltpu.make_async_copy(lift, lift_in, pair_sem.at[0]).wait()
        for k in range(2):
            pltpu.make_async_copy(part.at[pl.ds(4 * k, 4)], part_in.at[pl.ds(4 * k, 4)], pair_sem.at[2 + 2 * k]).wait()
        await_bytes(data_in.at[pl.ds(0, 31), pl.ds(0, 16)], send_sem.at[2])
        await_bytes(meta_in.at[pl.ds(0, 15)], send_sem.at[0])
        await_bytes(data_in.at[pl.ds(0, 15)], send_sem.at[1])

    @pl.when(jnp.logical_not(is_worker))
    def _():
        await_bytes(meta_in.at[pl.ds(0, 16)], send_sem.at[0])
        await_bytes(data_in.at[pl.ds(0, 16)], send_sem.at[1])


def body(samples, omega, points, ranks, pivots):
    anywhere = pl.BlockSpec(memory_space=pl.ANY)
    return pl.pallas_call(
        kernel,
        out_shape=pltpu.VMEM((1, 32, 1024), BF),
        in_specs=[anywhere] * 5,
        out_specs=pl.BlockSpec(memory_space=pltpu.VMEM),
        scratch_shapes=[
            pltpu.VMEM((8, 32), BF),
            pltpu.VMEM((2, 1, 512), I32),
            pltpu.SMEM((3, 32), I32),
            pltpu.VMEM((32, 1024), BF),
            pltpu.VMEM((32, 1024), BF),
            pltpu.VMEM((16, 32, 128), BF),
            pltpu.VMEM((1, 512), F32),
            pltpu.VMEM((32, 1, 512), F32),
            pltpu.VMEM((16, 8, 128), F32),
            pltpu.VMEM((32, 32, 128), BF),
            pltpu.VMEM((512, 1024), BF),
            pltpu.VMEM((512, 1024), BF),
            pltpu.VMEM((64, 128), BF),
            pltpu.VMEM((64, 128), BF),
            pltpu.VMEM((8, 16, 128), F32),
            pltpu.VMEM((8, 16, 128), F32),
            pltpu.VMEM((8, 16, 128), BF),
            pltpu.VMEM((16, 16, 128), BF),
            pltpu.SemaphoreType.DMA((5,)),
            pltpu.SemaphoreType.DMA((3,)),
            pltpu.SemaphoreType.DMA((3,)),
            pltpu.SemaphoreType.DMA((6,)),
        ],
        compiler_params=pltpu.CompilerParams(
            collective_id=0, has_side_effects=True, vmem_limit_bytes=60 * 2**20
        ),
        cost_estimate=pl.CostEstimate(flops=300_000_000, bytes_accessed=200_000, transcendentals=524288),
    )(samples, omega, points[:, 0, :], ranks, pivots)


def solution(mesh):
    return jax.shard_map(
        body,
        mesh=mesh,
        in_specs=(
            P("leaf", "grid", None),
            P("leaf", "grid", None),
            P(None, "leaf", "grid"),
            P(),
            P(None, "leaf", None),
        ),
        out_specs=P("leaf", "grid", None),
        check_vma=False,
    )
```

```python
import functools
import math

import jax
import jax.numpy as jnp
from jax import lax
from jax.experimental import pallas as pl
from jax.experimental.pallas import tpu as pltpu
from jax.sharding import PartitionSpec as P

MESH = pl.DeviceIdType.MESH
BF = jnp.bfloat16
F32 = jnp.float32
I32 = jnp.int32
kernel_rate = 0.6

NEAR = [3, 7, 4, 2, 1, 6, 10, 14, 9, 13, 8, 16, 19, 22, 20, 17]
MIDDLE = [p * 8 + c for p in (0, 3) for c in range(8)]
PLANES = [1, 3, 0, 2]
FAR_FIRST = sorted(range(32), key=lambda c: -(c // 8 * 10 + min(c // 2 % 4, 4 - c // 2 % 4) * 2 + c % 2))
OUT_ORDER = [[p * 8 + c for p in range(4) for c in cs] for cs in ((0, 2, 1, 3), (6, 4, 7, 5))]


def total(flags):
    return functools.reduce(lambda a, b: a + b, flags)


def kernel(
    samples, omega, points, ranks, pivots, out,
    pts_v, piv_v, rank_s, om_v, sa_v, packed, meta_out, meta_in, meta_turn, data_in, pick, mat, lift, lift_in, part, part_in,
    blocks, pieces,
    local_sem, send_sem, recv_sem, pair_sem,
):
    leaf = lax.axis_index("leaf")
    grid = lax.axis_index("grid")
    core = grid % 2
    x = grid // 4
    y = (grid // 2) % 2
    z = leaf % 4
    base = leaf - z
    back = (leaf % 16) // 8
    plane = total([jnp.where(z == k + back * (PLANES[k] - k), k, 0) for k in range(4)])
    chip = plane * 8 + x * 2 + y

    def device(number):
        cx, cy, cz = number // 2 % 4, number % 2, number // 8
        return (base + cz + back * (PLANES[cz] - cz), cx * 4 + cy * 2 + core)

    def worker(w):
        a, b = NEAR[w], MIDDLE[w]
        plane_a, plane_b = a // 8, PLANES[b // 8]
        return (base + plane_a + back * (plane_b - plane_a), (a % 8 + back * (b % 8 - a % 8)) * 2 + core)

    worker_chips = [a + back * (b - a) for a, b in zip(NEAR, MIDDLE, strict=True)]
    mine = total([jnp.where(chip == c, i + 1, 0) for i, c in enumerate(worker_chips)])
    is_worker = mine > 0
    slot = jnp.maximum(mine - 1, 0)
    meta_slot = chip % 4 * 8 + chip // 4
    peer = (leaf, grid + 1 - 2 * core)

    loads = [
        pltpu.make_async_copy(points, pts_v, local_sem.at[0]),
        pltpu.make_async_copy(pivots, piv_v, local_sem.at[1]),
        pltpu.make_async_copy(ranks, rank_s, local_sem.at[2]),
    ]
    bulk = [
        pltpu.make_async_copy(omega.at[0], om_v, local_sem.at[3]),
        pltpu.make_async_copy(samples.at[0], sa_v, local_sem.at[4]),
    ]
    for load in loads + bulk:
        load.start()

    barrier = pltpu.get_barrier_semaphore()

    @pl.when(is_worker)
    def _():
        for number in FAR_FIRST[::-1]:

            @pl.when(chip != number)
            def _():
                pl.semaphore_signal(barrier, inc=1, device_id=device(number), device_id_type=MESH)

        pl.semaphore_signal(barrier, inc=1, device_id=peer, device_id_type=MESH)

    for load in loads:
        load.wait()

    first_rank = rank_s[0, leaf]
    kept_rank = rank_s[1, leaf]
    child = (z // 2) % 2
    first_pivots = piv_v[0]
    last_pivots = piv_v[1]
    row = lax.broadcasted_iota(I32, (32, 512), 0)
    lane = lax.broadcasted_iota(I32, (32, 512), 1)
    own_row = (z % 2) * 512 + grid * 32 + row
    place = jnp.sum(jnp.where(first_pivots == own_row, lane + 1, 0).astype(F32), axis=1, keepdims=True)
    target = jnp.where(place > 0.5, child.astype(F32) * 512.0 + place - 1.0, -1.0)
    final = (
        jnp.sum(jnp.where(last_pivots.astype(F32) == target, lane + 1, 0).astype(F32), axis=1, keepdims=True) - 1.0
    )
    column = lax.broadcasted_iota(I32, (32, 1), 0)
    alive = (grid * 32 + column < first_rank).astype(F32)
    kept = alive * ((place > 0.5) & (place < kept_rank.astype(F32) + 0.5)).astype(F32)
    side = child.astype(F32)
    high = jnp.floor((final + 1.0) * (1.0 / 32.0))
    low = final + 1.0 - 32.0 * high
    field = lax.broadcasted_iota(I32, (32, 128), 1)
    fields = jnp.where(field == 11, side, 0.0)
    fields = jnp.where(field == 12, alive * (1.0 - side) + kept, fields)
    fields = jnp.where(field == 13, alive * (2.0 * side - 1.0), fields)
    fields = jnp.where(field == 14, high, fields)
    fields = jnp.where(field == 15, low, fields)
    coords = pts_v[...].astype(F32)
    norm = jnp.sum(coords * coords, axis=0, keepdims=True)
    norm_a = norm.astype(BF).astype(F32)
    norm_b = (norm - norm_a).astype(BF).astype(F32)
    norm_c = norm - norm_a - norm_b
    sub = lax.broadcasted_iota(I32, (8, 32), 0)
    norms = jnp.where(sub == 0, norm_a, jnp.where(sub == 1, norm_b, jnp.where(sub == 2, norm_c, 0.0)))
    upper = jnp.concatenate([coords, norms], axis=0).astype(BF)
    repeat = (
        lax.broadcasted_iota(I32, (32, 128), 1) % 32 == lax.broadcasted_iota(I32, (32, 128), 0)
    ).astype(BF)
    tile = jnp.dot(upper, repeat, preferred_element_type=F32)
    lower = lax.dot_general(fields.astype(BF), repeat, (((0,), (0,)), ((), ())), preferred_element_type=F32)
    tile = tile + lower[0:16]
    at_field = lax.broadcasted_iota(I32, (16, 128), 0)
    at_block = lax.broadcasted_iota(I32, (16, 128), 1) // 32
    for part_of in range(4):
        chosen_row = jnp.where(at_field == 4 * part_of + (at_block + 4 - chip % 4) % 4, tile, 0.0)
        meta_out[:, 128 * part_of : 128 * part_of + 128] = jnp.sum(chosen_row, axis=0, keepdims=True)

    @pl.when(is_worker)
    def _():
        pltpu.make_async_copy(meta_out, meta_in.at[meta_slot], recv_sem.at[0]).start()

    pl.semaphore_wait(barrier, 16)

    def send_all(source, target, number, order=tuple(range(16))):
        for w in order:

            @pl.when(chip != worker_chips[w])
            def _():
                pltpu.make_async_remote_copy(
                    src_ref=source(w),
                    dst_ref=target,
                    send_sem=send_sem.at[number],
                    recv_sem=recv_sem.at[number],
                    device_id=worker(w),
                    device_id_type=MESH,
                ).start()

    send_all(lambda w: meta_out, meta_in.at[meta_slot], 0)
    for load in bulk:
        load.wait()

    left_half = lax.broadcasted_iota(I32, (32, 128), 1) < 64
    for v in range(8):
        o = om_v[:, 128 * v : 128 * v + 128].astype(F32)
        a = sa_v[:, 128 * v : 128 * v + 128].astype(F32)
        packed[2 * v] = jnp.where(left_half, o, pltpu.roll(a, 64, 1)).astype(BF)
        packed[2 * v + 1] = jnp.where(left_half, pltpu.roll(o, 64, 1), a).astype(BF)

    @pl.when(is_worker)
    def _():
        pltpu.make_async_copy(packed.at[slot], data_in.at[chip], recv_sem.at[1]).start()

    @pl.when(chip % 2 == 0)
    def _():
        send_all(lambda w: packed.at[w], data_in.at[chip], 1)

    @pl.when(chip % 2 == 1)
    def _():
        send_all(lambda w: packed.at[w], data_in.at[chip], 1, tuple(range(8, 16)) + tuple(range(8)))

    def await_bytes(ref, sem):
        pltpu.make_async_copy(ref, ref, sem).wait()

    @pl.when(is_worker)
    def _():
        await_bytes(meta_in, recv_sem.at[0])
        block = lax.broadcasted_iota(I32, (8, 128), 1) // 32
        for f in range(16):
            turned = meta_in[0:8, 0, f // 4 * 128 : f // 4 * 128 + 128]
            for q in range(1, 4):
                source = meta_in[8 * q : 8 * q + 8, 0, f // 4 * 128 : f // 4 * 128 + 128]
                turned = jnp.where(block == (q + f % 4) % 4, source, turned)
            turned = pltpu.roll(turned, (4 - f % 4) * 32, 1) if f % 4 else turned
            meta_turn[f] = turned
        meta = jnp.concatenate([meta_turn[:, group, :] for group in range(8)], axis=1)
        position = meta[14:15] * 32.0 + meta[15:16] - 1.0
        part_row = lax.broadcasted_iota(I32, (16, 1024), 0)
        right = jnp.where(part_row < 11, meta, jnp.where(part_row < 14, 1.0, 0.0)).astype(BF)
        shift = jnp.concatenate([meta[13:16], meta[0:13]], axis=0)
        raised = jnp.where(
            part_row < 8, -2.0 * meta, jnp.where((part_row >= 11) & (part_row < 14), shift, 0.0)
        )
        raised = jnp.where(part_row == 14, meta[11:12], raised).astype(BF)
        factor = jnp.where(part_row == 14, meta[13:14], jnp.where(part_row == 15, meta[12:13], 0.0)).astype(BF)

        eight = jnp.concatenate([raised] * 8, axis=0)
        chunk_lane = lax.broadcasted_iota(I32, (64, 128), 1) // 16
        gathered = [None, None]
        swaps = [None, None]
        for k in (1, 0):
            half = core if k else 1 - core
            for chunk in range(4 * k, 4 * k + 4):
                line = lax.broadcasted_iota(I32, (64, 1), 0) + 64 * (chunk % 4)
                order = line // 32 * 64 + half * 32 + line % 32
                hit = (position == order.astype(F32)).astype(BF)
                pick[pl.ds(64 * chunk, 64), :] = hit
            picked = lax.dot_general(
                pick[256 * k : 256 * k + 256], eight, (((1,), (1,)), ((), ())), preferred_element_type=F32
            )
            gathered[k] = total(
                [jnp.where(chunk_lane == 4 * k + g, picked[64 * g : 64 * g + 64], 0.0) for g in range(4)]
            )
            lift[1 - k] = pltpu.roll(gathered[k], 64, 1).astype(BF)
            swaps[1 - k] = pltpu.make_async_remote_copy(
                src_ref=lift.at[1 - k], dst_ref=lift_in.at[1 - k],
                send_sem=pair_sem.at[6 - 6 * k], recv_sem=pair_sem.at[7 - 6 * k],
                device_id=peer, device_id_type=MESH,
            )
            swaps[1 - k].start()
        right = jnp.concatenate([right] * 8, axis=0)
        factor = jnp.concatenate([factor] * 8, axis=0)
        spread = lax.broadcasted_iota(I32, (64, 128), 1) % 16
        ones = jnp.where(((spread >= 8) & (spread < 11)) | (spread == 15), 1.0, 0.0)

        def selected(k):
            swaps[k].wait_recv()
            return gathered[k] + lift_in[k].astype(F32) + ones

        scale = -kernel_rate * math.log2(math.e)

        def form(chunk, left):
            rows = slice(64 * chunk, 64 * chunk + 64)
            one = jnp.where(chunk_lane == chunk, left, 0.0).astype(BF)
            distance = jnp.dot(one, right, preferred_element_type=F32)
            coef = jnp.dot(one, factor, preferred_element_type=F32)
            diagonal = pick[rows, :].astype(F32)
            entry = (jnp.exp2(distance * scale) + diagonal).astype(BF)
            mat[rows, :] = entry * coef.astype(BF)

        left_lanes = lax.broadcasted_iota(I32, (8, 16, 128), 2) < 64

        def combine(first, count):
            rows = slice(first, first + 32 * count)
            data = data_in[...].reshape(1024, 128)
            chosen = jnp.dot(pick[rows], data, preferred_element_type=F32).reshape(count, 32, 128)
            product = jnp.dot(mat[rows], data, preferred_element_type=F32).reshape(count, 32, 128)
            above = pltpu.roll(chosen[:, 0:16], 64, 2) - product[:, 0:16]
            below = chosen[:, 16:32] - pltpu.roll(product[:, 16:32], 64, 2)
            return jnp.where(left_lanes[0:count], above, below)

        left = selected(0)
        for chunk in range(4):
            form(chunk, left)
        await_bytes(data_in, recv_sem.at[1])
        trades = []
        for k in range(2):
            part[4 * k : 4 * k + 4] = combine(128 * k, 4)
            trade = pltpu.make_async_remote_copy(
                src_ref=part.at[pl.ds(4 * k, 4)], dst_ref=part_in.at[pl.ds(4 * k, 4)],
                send_sem=pair_sem.at[2 + 2 * k], recv_sem=pair_sem.at[3 + 2 * k],
                device_id=peer, device_id_type=MESH,
            )
            trade.start()
            trades.append(trade)
        left = selected(1)
        for chunk in range(4, 8):
            form(chunk, left)
        mine_rows = combine(256, 8)
        last_rank = rank_s[2, leaf]
        order = (
            lax.broadcasted_iota(I32, (8, 16, 128), 0) * 64 + core * 32
            + jnp.where(left_lanes, 0, 16) + lax.broadcasted_iota(I32, (8, 16, 128), 1)
        )
        for k in range(2):
            trades[k].wait_recv()
            these = slice(4 * k, 4 * k + 4)
            blocks[these] = jnp.where(order[these] < last_rank, mine_rows[these] + part_in[these], 0.0).astype(BF)
            for number in OUT_ORDER[k]:
                block = blocks.at[number % 8]

                @pl.when(chip != number)
                def _():
                    pltpu.make_async_remote_copy(
                        src_ref=block,
                        dst_ref=pieces.at[slot],
                        send_sem=send_sem.at[2],
                        recv_sem=recv_sem.at[2],
                        device_id=device(number),
                        device_id_type=MESH,
                    ).start()

        pltpu.make_async_copy(blocks.at[x * 2 + y], pieces.at[slot], recv_sem.at[2]).start()

    await_bytes(pieces, recv_sem.at[2])
    left_part = lax.broadcasted_iota(I32, (16, 128), 1) < 64
    for v in range(8):
        even = pieces[2 * v].astype(F32)
        odd = pieces[2 * v + 1].astype(F32)
        columns = slice(128 * v, 128 * v + 128)
        out[0, 0:16, columns] = jnp.where(left_part, even, pltpu.roll(odd, 64, 1)).astype(BF)
        out[0, 16:32, columns] = jnp.where(left_part, pltpu.roll(even, 64, 1), odd).astype(BF)

    @pl.when(is_worker)
    def _():
        for k in range(2):
            pltpu.make_async_copy(lift.at[k], lift_in.at[k], pair_sem.at[6 * k]).wait()
        for k in range(2):
            pltpu.make_async_copy(part.at[pl.ds(4 * k, 4)], part_in.at[pl.ds(4 * k, 4)], pair_sem.at[2 + 2 * k]).wait()
        await_bytes(data_in.at[pl.ds(0, 31), pl.ds(0, 16)], send_sem.at[2])
        await_bytes(meta_in.at[pl.ds(0, 15)], send_sem.at[0])
        await_bytes(data_in.at[pl.ds(0, 15)], send_sem.at[1])

    @pl.when(jnp.logical_not(is_worker))
    def _():
        await_bytes(meta_in.at[pl.ds(0, 16)], send_sem.at[0])
        await_bytes(data_in.at[pl.ds(0, 16)], send_sem.at[1])


def body(samples, omega, points, ranks, pivots):
    anywhere = pl.BlockSpec(memory_space=pl.ANY)
    return pl.pallas_call(
        kernel,
        out_shape=pltpu.VMEM((1, 32, 1024), BF),
        in_specs=[anywhere] * 5,
        out_specs=pl.BlockSpec(memory_space=pltpu.VMEM),
        scratch_shapes=[
            pltpu.VMEM((8, 32), BF),
            pltpu.VMEM((2, 1, 512), I32),
            pltpu.SMEM((3, 32), I32),
            pltpu.VMEM((32, 1024), BF),
            pltpu.VMEM((32, 1024), BF),
            pltpu.VMEM((16, 32, 128), BF),
            pltpu.VMEM((1, 512), F32),
            pltpu.VMEM((32, 1, 512), F32),
            pltpu.VMEM((16, 8, 128), F32),
            pltpu.VMEM((32, 32, 128), BF),
            pltpu.VMEM((512, 1024), BF),
            pltpu.VMEM((512, 1024), BF),
            pltpu.VMEM((2, 64, 128), BF),
            pltpu.VMEM((2, 64, 128), BF),
            pltpu.VMEM((8, 16, 128), F32),
            pltpu.VMEM((8, 16, 128), F32),
            pltpu.VMEM((8, 16, 128), BF),
            pltpu.VMEM((16, 16, 128), BF),
            pltpu.SemaphoreType.DMA((5,)),
            pltpu.SemaphoreType.DMA((3,)),
            pltpu.SemaphoreType.DMA((3,)),
            pltpu.SemaphoreType.DMA((8,)),
        ],
        compiler_params=pltpu.CompilerParams(
            collective_id=0, has_side_effects=True, vmem_limit_bytes=60 * 2**20
        ),
        cost_estimate=pl.CostEstimate(flops=300_000_000, bytes_accessed=200_000, transcendentals=524288),
    )(samples, omega, points[:, 0, :], ranks, pivots)


def solution(mesh):
    return jax.shard_map(
        body,
        mesh=mesh,
        in_specs=(
            P("leaf", "grid", None),
            P("leaf", "grid", None),
            P(None, "leaf", "grid"),
            P(),
            P(None, "leaf", None),
        ),
        out_specs=P("leaf", "grid", None),
        check_vma=False,
    )
```

```python
import functools
import math

import jax
import jax.numpy as jnp
from jax import lax
from jax.experimental import pallas as pl
from jax.experimental.pallas import tpu as pltpu
from jax.sharding import PartitionSpec as P

MESH = pl.DeviceIdType.MESH
BF = jnp.bfloat16
F32 = jnp.float32
I32 = jnp.int32
kernel_rate = 0.6

NEAR = [3, 7, 4, 2, 1, 6, 10, 14, 9, 13, 8, 16, 19, 22, 20, 17]
MIDDLE = [p * 8 + c for p in (0, 3) for c in range(8)]
PLANES = [1, 3, 0, 2]
FAR_FIRST = sorted(range(32), key=lambda c: -(c // 8 * 10 + min(c // 2 % 4, 4 - c // 2 % 4) * 2 + c % 2))
OUT_ORDER = [[p * 8 + c for p in range(4) for c in cs] for cs in ((0, 2, 1, 3), (6, 4, 7, 5))]


def total(flags):
    return functools.reduce(lambda a, b: a + b, flags)


def kernel(
    samples, omega, points, ranks, pivots, out,
    pts_v, piv_v, rank_s, om_v, sa_v, packed, meta_out, meta_in, meta_turn, data_in, pick, mat, lift, lift_in, part, part_in,
    blocks, pieces,
    local_sem, send_sem, recv_sem, pair_sem,
):
    leaf = lax.axis_index("leaf")
    grid = lax.axis_index("grid")
    core = grid % 2
    x = grid // 4
    y = (grid // 2) % 2
    z = leaf % 4
    base = leaf - z
    back = (leaf % 16) // 8
    plane = total([jnp.where(z == k + back * (PLANES[k] - k), k, 0) for k in range(4)])
    chip = plane * 8 + x * 2 + y

    def device(number):
        cx, cy, cz = number // 2 % 4, number % 2, number // 8
        return (base + cz + back * (PLANES[cz] - cz), cx * 4 + cy * 2 + core)

    def worker(w):
        a, b = NEAR[w], MIDDLE[w]
        plane_a, plane_b = a // 8, PLANES[b // 8]
        return (base + plane_a + back * (plane_b - plane_a), (a % 8 + back * (b % 8 - a % 8)) * 2 + core)

    worker_chips = [a + back * (b - a) for a, b in zip(NEAR, MIDDLE, strict=True)]
    mine = total([jnp.where(chip == c, i + 1, 0) for i, c in enumerate(worker_chips)])
    is_worker = mine > 0
    slot = jnp.maximum(mine - 1, 0)
    meta_slot = chip % 4 * 8 + chip // 4
    peer = (leaf, grid + 1 - 2 * core)

    loads = [
        pltpu.make_async_copy(points, pts_v, local_sem.at[0]),
        pltpu.make_async_copy(pivots, piv_v, local_sem.at[1]),
        pltpu.make_async_copy(ranks, rank_s, local_sem.at[2]),
    ]
    bulk = [
        pltpu.make_async_copy(omega.at[0], om_v, local_sem.at[3]),
        pltpu.make_async_copy(samples.at[0], sa_v, local_sem.at[4]),
    ]
    for load in loads + bulk:
        load.start()

    barrier = pltpu.get_barrier_semaphore()

    @pl.when(is_worker)
    def _():
        for number in FAR_FIRST[::-1]:

            @pl.when(chip != number)
            def _():
                pl.semaphore_signal(barrier, inc=1, device_id=device(number), device_id_type=MESH)

        pl.semaphore_signal(barrier, inc=1, device_id=peer, device_id_type=MESH)

    for load in loads:
        load.wait()

    first_rank = rank_s[0, leaf]
    kept_rank = rank_s[1, leaf]
    child = (z // 2) % 2
    first_pivots = piv_v[0]
    last_pivots = piv_v[1]
    row = lax.broadcasted_iota(I32, (32, 512), 0)
    lane = lax.broadcasted_iota(I32, (32, 512), 1)
    own_row = (z % 2) * 512 + grid * 32 + row
    place = jnp.sum(jnp.where(first_pivots == own_row, lane + 1, 0).astype(F32), axis=1, keepdims=True)
    target = jnp.where(place > 0.5, child.astype(F32) * 512.0 + place - 1.0, -1.0)
    final = (
        jnp.sum(jnp.where(last_pivots.astype(F32) == target, lane + 1, 0).astype(F32), axis=1, keepdims=True) - 1.0
    )
    column = lax.broadcasted_iota(I32, (32, 1), 0)
    alive = (grid * 32 + column < first_rank).astype(F32)
    kept = alive * ((place > 0.5) & (place < kept_rank.astype(F32) + 0.5)).astype(F32)
    side = child.astype(F32)
    high = jnp.floor((final + 1.0) * (1.0 / 32.0))
    low = final + 1.0 - 32.0 * high
    field = lax.broadcasted_iota(I32, (32, 128), 1)
    fields = jnp.where(field == 11, side, 0.0)
    fields = jnp.where(field == 12, alive * (1.0 - side) + kept, fields)
    fields = jnp.where(field == 13, alive * (2.0 * side - 1.0), fields)
    fields = jnp.where(field == 14, high, fields)
    fields = jnp.where(field == 15, low, fields)
    coords = pts_v[...].astype(F32)
    norm = jnp.sum(coords * coords, axis=0, keepdims=True)
    norm_a = norm.astype(BF).astype(F32)
    norm_b = (norm - norm_a).astype(BF).astype(F32)
    norm_c = norm - norm_a - norm_b
    sub = lax.broadcasted_iota(I32, (8, 32), 0)
    norms = jnp.where(sub == 0, norm_a, jnp.where(sub == 1, norm_b, jnp.where(sub == 2, norm_c, 0.0)))
    upper = jnp.concatenate([coords, norms], axis=0).astype(BF)
    repeat = (
        lax.broadcasted_iota(I32, (32, 128), 1) % 32 == lax.broadcasted_iota(I32, (32, 128), 0)
    ).astype(BF)
    tile = jnp.dot(upper, repeat, preferred_element_type=F32)
    lower = lax.dot_general(fields.astype(BF), repeat, (((0,), (0,)), ((), ())), preferred_element_type=F32)
    tile = tile + lower[0:16]
    at_field = lax.broadcasted_iota(I32, (16, 128), 0)
    at_block = lax.broadcasted_iota(I32, (16, 128), 1) // 32
    for part_of in range(4):
        chosen_row = jnp.where(at_field == 4 * part_of + (at_block + 4 - chip % 4) % 4, tile, 0.0)
        meta_out[:, 128 * part_of : 128 * part_of + 128] = jnp.sum(chosen_row, axis=0, keepdims=True)

    @pl.when(is_worker)
    def _():
        pltpu.make_async_copy(meta_out, meta_in.at[meta_slot], recv_sem.at[0]).start()

    pl.semaphore_wait(barrier, 16)

    def send_all(source, target, number, order=tuple(range(16))):
        for w in order:

            @pl.when(chip != worker_chips[w])
            def _():
                pltpu.make_async_remote_copy(
                    src_ref=source(w),
                    dst_ref=target,
                    send_sem=send_sem.at[number],
                    recv_sem=recv_sem.at[number],
                    device_id=worker(w),
                    device_id_type=MESH,
                ).start()

    send_all(lambda w: meta_out, meta_in.at[meta_slot], 0)
    for load in bulk:
        load.wait()

    left_half = lax.broadcasted_iota(I32, (32, 128), 1) < 64
    for v in range(8):
        o = om_v[:, 128 * v : 128 * v + 128].astype(F32)
        a = sa_v[:, 128 * v : 128 * v + 128].astype(F32)
        packed[2 * v] = jnp.where(left_half, o, pltpu.roll(a, 64, 1)).astype(BF)
        packed[2 * v + 1] = jnp.where(left_half, pltpu.roll(o, 64, 1), a).astype(BF)

    @pl.when(is_worker)
    def _():
        pltpu.make_async_copy(packed.at[slot], data_in.at[chip], recv_sem.at[1]).start()

    @pl.when(chip % 2 == 0)
    def _():
        send_all(lambda w: packed.at[w], data_in.at[chip], 1)

    @pl.when(chip % 2 == 1)
    def _():
        send_all(lambda w: packed.at[w], data_in.at[chip], 1, tuple(range(8, 16)) + tuple(range(8)))

    def await_bytes(ref, sem):
        pltpu.make_async_copy(ref, ref, sem).wait()

    @pl.when(is_worker)
    def _():
        await_bytes(meta_in, recv_sem.at[0])
        block = lax.broadcasted_iota(I32, (8, 128), 1) // 32
        for f in range(16):
            turned = meta_in[0:8, 0, f // 4 * 128 : f // 4 * 128 + 128]
            for q in range(1, 4):
                source = meta_in[8 * q : 8 * q + 8, 0, f // 4 * 128 : f // 4 * 128 + 128]
                turned = jnp.where(block == (q + f % 4) % 4, source, turned)
            turned = pltpu.roll(turned, (4 - f % 4) * 32, 1) if f % 4 else turned
            meta_turn[f] = turned
        meta = jnp.concatenate([meta_turn[:, group, :] for group in range(8)], axis=1)
        position = meta[14:15] * 32.0 + meta[15:16] - 1.0
        part_row = lax.broadcasted_iota(I32, (16, 1024), 0)
        right = jnp.where(part_row < 11, meta, jnp.where(part_row < 14, 1.0, 0.0)).astype(BF)
        shift = jnp.concatenate([meta[13:16], meta[0:13]], axis=0)
        raised = jnp.where(
            part_row < 8, -2.0 * meta, jnp.where((part_row >= 11) & (part_row < 14), shift, 0.0)
        )
        raised = jnp.where(part_row == 14, meta[11:12], raised).astype(BF)
        factor = jnp.where(part_row == 14, meta[13:14], jnp.where(part_row == 15, meta[12:13], 0.0)).astype(BF)

        eight = jnp.concatenate([raised] * 8, axis=0)
        chunk_lane = lax.broadcasted_iota(I32, (64, 128), 1) // 16
        gathered = [None, None]
        swaps = [None, None]
        for k in (1, 0):
            half = core if k else 1 - core
            for chunk in range(4 * k, 4 * k + 4):
                line = lax.broadcasted_iota(I32, (64, 1), 0) + 64 * (chunk % 4)
                order = line // 32 * 64 + half * 32 + line % 32
                hit = (position == order.astype(F32)).astype(BF)
                pick[pl.ds(64 * chunk, 64), :] = hit
            picked = lax.dot_general(
                pick[256 * k : 256 * k + 256], eight, (((1,), (1,)), ((), ())), preferred_element_type=F32
            )
            gathered[k] = total(
                [jnp.where(chunk_lane == 4 * k + g, picked[64 * g : 64 * g + 64], 0.0) for g in range(4)]
            )
            lift[1 - k] = pltpu.roll(gathered[k], 64, 1).astype(BF)
            swaps[1 - k] = pltpu.make_async_remote_copy(
                src_ref=lift.at[1 - k], dst_ref=lift_in.at[1 - k],
                send_sem=pair_sem.at[6 - 6 * k], recv_sem=pair_sem.at[7 - 6 * k],
                device_id=peer, device_id_type=MESH,
            )
            swaps[1 - k].start()
        right = jnp.concatenate([right] * 8, axis=0)
        factor = jnp.concatenate([factor] * 8, axis=0)
        spread = lax.broadcasted_iota(I32, (64, 128), 1) % 16
        ones = jnp.where(((spread >= 8) & (spread < 11)) | (spread == 15), 1.0, 0.0)

        def selected(k):
            swaps[k].wait_recv()
            return gathered[k] + lift_in[k].astype(F32) + ones

        scale = -kernel_rate * math.log2(math.e)

        def form(chunk, left):
            rows = slice(64 * chunk, 64 * chunk + 64)
            one = jnp.where(chunk_lane == chunk, left, 0.0).astype(BF)
            distance = jnp.dot(one, right, preferred_element_type=F32)
            coef = jnp.dot(one, factor, preferred_element_type=F32)
            diagonal = pick[rows, :].astype(F32)
            entry = (jnp.exp2(distance * scale) + diagonal).astype(BF)
            mat[rows, :] = entry * coef.astype(BF)

        left_lanes = lax.broadcasted_iota(I32, (8, 16, 128), 2) < 64

        def combine(first, count):
            rows = slice(first, first + 32 * count)
            data = data_in[...].reshape(1024, 128)
            chosen = jnp.dot(pick[rows], data, preferred_element_type=F32).reshape(count, 32, 128)
            product = jnp.dot(mat[rows], data, preferred_element_type=F32).reshape(count, 32, 128)
            above = pltpu.roll(chosen[:, 0:16], 64, 2) - product[:, 0:16]
            below = chosen[:, 16:32] - pltpu.roll(product[:, 16:32], 64, 2)
            return jnp.where(left_lanes[0:count], above, below)

        left = selected(0)
        for chunk in range(4):
            form(chunk, left)
        await_bytes(data_in, recv_sem.at[1])
        trades = []
        for k in range(2):
            part[4 * k : 4 * k + 4] = combine(128 * k, 4)
            trade = pltpu.make_async_remote_copy(
                src_ref=part.at[pl.ds(4 * k, 4)], dst_ref=part_in.at[pl.ds(4 * k, 4)],
                send_sem=pair_sem.at[2 + 2 * k], recv_sem=pair_sem.at[3 + 2 * k],
                device_id=peer, device_id_type=MESH,
            )
            trade.start()
            trades.append(trade)
        left = selected(1)
        for chunk in range(4, 8):
            form(chunk, left)
        mine_rows = combine(256, 8)
        last_rank = rank_s[2, leaf]
        order = (
            lax.broadcasted_iota(I32, (8, 16, 128), 0) * 64 + core * 32
            + jnp.where(left_lanes, 0, 16) + lax.broadcasted_iota(I32, (8, 16, 128), 1)
        )
        for k in range(2):
            trades[k].wait_recv()
            these = slice(4 * k, 4 * k + 4)
            blocks[these] = jnp.where(order[these] < last_rank, mine_rows[these] + part_in[these], 0.0).astype(BF)
            for number in OUT_ORDER[k]:
                block = blocks.at[number % 8]

                @pl.when(chip != number)
                def _():
                    pltpu.make_async_remote_copy(
                        src_ref=block,
                        dst_ref=pieces.at[slot],
                        send_sem=send_sem.at[2],
                        recv_sem=recv_sem.at[2 + slot // 8],
                        device_id=device(number),
                        device_id_type=MESH,
                    ).start()

        pltpu.make_async_copy(blocks.at[x * 2 + y], pieces.at[slot], recv_sem.at[2 + slot // 8]).start()

    left_part = lax.broadcasted_iota(I32, (16, 128), 1) < 64
    for v in range(8):
        if v % 4 == 0:
            await_bytes(pieces.at[pl.ds(2 * v, 8)], recv_sem.at[2 + v // 4])
        even = pieces[2 * v].astype(F32)
        odd = pieces[2 * v + 1].astype(F32)
        columns = slice(128 * v, 128 * v + 128)
        out[0, 0:16, columns] = jnp.where(left_part, even, pltpu.roll(odd, 64, 1)).astype(BF)
        out[0, 16:32, columns] = jnp.where(left_part, pltpu.roll(even, 64, 1), odd).astype(BF)

    @pl.when(is_worker)
    def _():
        for k in range(2):
            pltpu.make_async_copy(lift.at[k], lift_in.at[k], pair_sem.at[6 * k]).wait()
        for k in range(2):
            pltpu.make_async_copy(part.at[pl.ds(4 * k, 4)], part_in.at[pl.ds(4 * k, 4)], pair_sem.at[2 + 2 * k]).wait()
        await_bytes(data_in.at[pl.ds(0, 31), pl.ds(0, 16)], send_sem.at[2])
        await_bytes(meta_in.at[pl.ds(0, 15)], send_sem.at[0])
        await_bytes(data_in.at[pl.ds(0, 15)], send_sem.at[1])

    @pl.when(jnp.logical_not(is_worker))
    def _():
        await_bytes(meta_in.at[pl.ds(0, 16)], send_sem.at[0])
        await_bytes(data_in.at[pl.ds(0, 16)], send_sem.at[1])


def body(samples, omega, points, ranks, pivots):
    anywhere = pl.BlockSpec(memory_space=pl.ANY)
    return pl.pallas_call(
        kernel,
        out_shape=pltpu.VMEM((1, 32, 1024), BF),
        in_specs=[anywhere] * 5,
        out_specs=pl.BlockSpec(memory_space=pltpu.VMEM),
        scratch_shapes=[
            pltpu.VMEM((8, 32), BF),
            pltpu.VMEM((2, 1, 512), I32),
            pltpu.SMEM((3, 32), I32),
            pltpu.VMEM((32, 1024), BF),
            pltpu.VMEM((32, 1024), BF),
            pltpu.VMEM((16, 32, 128), BF),
            pltpu.VMEM((1, 512), F32),
            pltpu.VMEM((32, 1, 512), F32),
            pltpu.VMEM((16, 8, 128), F32),
            pltpu.VMEM((32, 32, 128), BF),
            pltpu.VMEM((512, 1024), BF),
            pltpu.VMEM((512, 1024), BF),
            pltpu.VMEM((2, 64, 128), BF),
            pltpu.VMEM((2, 64, 128), BF),
            pltpu.VMEM((8, 16, 128), F32),
            pltpu.VMEM((8, 16, 128), F32),
            pltpu.VMEM((8, 16, 128), BF),
            pltpu.VMEM((16, 16, 128), BF),
            pltpu.SemaphoreType.DMA((5,)),
            pltpu.SemaphoreType.DMA((3,)),
            pltpu.SemaphoreType.DMA((4,)),
            pltpu.SemaphoreType.DMA((8,)),
        ],
        compiler_params=pltpu.CompilerParams(
            collective_id=0, has_side_effects=True, vmem_limit_bytes=60 * 2**20
        ),
        cost_estimate=pl.CostEstimate(flops=300_000_000, bytes_accessed=200_000, transcendentals=524288),
    )(samples, omega, points[:, 0, :], ranks, pivots)


def solution(mesh):
    return jax.shard_map(
        body,
        mesh=mesh,
        in_specs=(
            P("leaf", "grid", None),
            P("leaf", "grid", None),
            P(None, "leaf", "grid"),
            P(),
            P(None, "leaf", None),
        ),
        out_specs=P("leaf", "grid", None),
        check_vma=False,
    )
```

```python
import functools
import math

import jax
import jax.numpy as jnp
from jax import lax
from jax.experimental import pallas as pl
from jax.experimental.pallas import tpu as pltpu
from jax.sharding import PartitionSpec as P

MESH = pl.DeviceIdType.MESH
BF = jnp.bfloat16
F32 = jnp.float32
I32 = jnp.int32
kernel_rate = 0.6

NEAR = [3, 7, 4, 2, 1, 6, 10, 14, 9, 13, 8, 16, 19, 22, 20, 17]
MIDDLE = [p * 8 + c for p in (0, 3) for c in range(8)]
PLANES = [1, 3, 0, 2]
FAR_FIRST = sorted(range(32), key=lambda c: -(c // 8 * 10 + min(c // 2 % 4, 4 - c // 2 % 4) * 2 + c % 2))
OUT_ORDER = [[p * 8 + c for p in range(4) for c in cs] for cs in ((0, 2, 1, 3), (6, 4, 7, 5))]


def total(flags):
    return functools.reduce(lambda a, b: a + b, flags)


def kernel(
    samples, omega, points, ranks, pivots, out,
    pts_v, piv_v, rank_s, om_v, sa_v, packed, meta_out, meta_in, meta_turn, data_in, pick, mat, lift, lift_in, part, part_in,
    blocks, pieces,
    local_sem, send_sem, recv_sem, pair_sem,
):
    leaf = lax.axis_index("leaf")
    grid = lax.axis_index("grid")
    core = grid % 2
    x = grid // 4
    y = (grid // 2) % 2
    z = leaf % 4
    base = leaf - z
    back = (leaf % 16) // 8
    plane = total([jnp.where(z == k + back * (PLANES[k] - k), k, 0) for k in range(4)])
    chip = plane * 8 + x * 2 + y

    def device(number):
        cx, cy, cz = number // 2 % 4, number % 2, number // 8
        return (base + cz + back * (PLANES[cz] - cz), cx * 4 + cy * 2 + core)

    def worker(w):
        a, b = NEAR[w], MIDDLE[w]
        plane_a, plane_b = a // 8, PLANES[b // 8]
        return (base + plane_a + back * (plane_b - plane_a), (a % 8 + back * (b % 8 - a % 8)) * 2 + core)

    worker_chips = [a + back * (b - a) for a, b in zip(NEAR, MIDDLE, strict=True)]
    mine = total([jnp.where(chip == c, i + 1, 0) for i, c in enumerate(worker_chips)])
    is_worker = mine > 0
    slot = jnp.maximum(mine - 1, 0)
    meta_slot = chip % 4 * 8 + chip // 4
    peer = (leaf, grid + 1 - 2 * core)

    loads = [
        pltpu.make_async_copy(points, pts_v, local_sem.at[0]),
        pltpu.make_async_copy(pivots, piv_v, local_sem.at[1]),
        pltpu.make_async_copy(ranks, rank_s, local_sem.at[2]),
    ]
    bulk = [
        pltpu.make_async_copy(omega.at[0], om_v, local_sem.at[3]),
        pltpu.make_async_copy(samples.at[0], sa_v, local_sem.at[4]),
    ]
    for load in loads + bulk:
        load.start()

    barrier = pltpu.get_barrier_semaphore()

    @pl.when(is_worker)
    def _():
        for number in FAR_FIRST[::-1]:

            @pl.when(chip != number)
            def _():
                pl.semaphore_signal(barrier, inc=1, device_id=device(number), device_id_type=MESH)

        pl.semaphore_signal(barrier, inc=1, device_id=peer, device_id_type=MESH)

    for load in loads:
        load.wait()

    first_rank = rank_s[0, leaf]
    kept_rank = rank_s[1, leaf]
    child = (z // 2) % 2
    first_pivots = piv_v[0]
    last_pivots = piv_v[1]
    row = lax.broadcasted_iota(I32, (32, 512), 0)
    lane = lax.broadcasted_iota(I32, (32, 512), 1)
    own_row = (z % 2) * 512 + grid * 32 + row
    place = jnp.sum(jnp.where(first_pivots == own_row, lane + 1, 0).astype(F32), axis=1, keepdims=True)
    target = jnp.where(place > 0.5, child.astype(F32) * 512.0 + place - 1.0, -1.0)
    final = (
        jnp.sum(jnp.where(last_pivots.astype(F32) == target, lane + 1, 0).astype(F32), axis=1, keepdims=True) - 1.0
    )
    column = lax.broadcasted_iota(I32, (32, 1), 0)
    alive = (grid * 32 + column < first_rank).astype(F32)
    kept = alive * ((place > 0.5) & (place < kept_rank.astype(F32) + 0.5)).astype(F32)
    side = child.astype(F32)
    high = jnp.floor((final + 1.0) * (1.0 / 32.0))
    low = final + 1.0 - 32.0 * high
    field = lax.broadcasted_iota(I32, (32, 128), 1)
    fields = jnp.where(field == 11, side, 0.0)
    fields = jnp.where(field == 12, alive * (1.0 - side) + kept, fields)
    fields = jnp.where(field == 13, alive * (2.0 * side - 1.0), fields)
    fields = jnp.where(field == 14, high, fields)
    fields = jnp.where(field == 15, low, fields)
    coords = pts_v[...].astype(F32)
    norm = jnp.sum(coords * coords, axis=0, keepdims=True)
    norm_a = norm.astype(BF).astype(F32)
    norm_b = (norm - norm_a).astype(BF).astype(F32)
    norm_c = norm - norm_a - norm_b
    sub = lax.broadcasted_iota(I32, (8, 32), 0)
    norms = jnp.where(sub == 0, norm_a, jnp.where(sub == 1, norm_b, jnp.where(sub == 2, norm_c, 0.0)))
    upper = jnp.concatenate([coords, norms], axis=0).astype(BF)
    repeat = (
        lax.broadcasted_iota(I32, (32, 128), 1) % 32 == lax.broadcasted_iota(I32, (32, 128), 0)
    ).astype(BF)
    tile = jnp.dot(upper, repeat, preferred_element_type=F32)
    lower = lax.dot_general(fields.astype(BF), repeat, (((0,), (0,)), ((), ())), preferred_element_type=F32)
    tile = tile + lower[0:16]
    at_field = lax.broadcasted_iota(I32, (16, 128), 0)
    at_block = lax.broadcasted_iota(I32, (16, 128), 1) // 32
    for part_of in range(4):
        chosen_row = jnp.where(at_field == 4 * part_of + (at_block + 4 - chip % 4) % 4, tile, 0.0)
        meta_out[:, 128 * part_of : 128 * part_of + 128] = jnp.sum(chosen_row, axis=0, keepdims=True)

    @pl.when(is_worker)
    def _():
        pltpu.make_async_copy(meta_out, meta_in.at[meta_slot], recv_sem.at[0]).start()

    pl.semaphore_wait(barrier, 16)

    def send_all(source, target, number, order=tuple(range(16))):
        for w in order:

            @pl.when(chip != worker_chips[w])
            def _():
                pltpu.make_async_remote_copy(
                    src_ref=source(w),
                    dst_ref=target,
                    send_sem=send_sem.at[number],
                    recv_sem=recv_sem.at[number],
                    device_id=worker(w),
                    device_id_type=MESH,
                ).start()

    send_all(lambda w: meta_out, meta_in.at[meta_slot], 0)
    for load in bulk:
        load.wait()

    left_half = lax.broadcasted_iota(I32, (32, 128), 1) < 64
    for v in range(8):
        o = om_v[:, 128 * v : 128 * v + 128].astype(F32)
        a = sa_v[:, 128 * v : 128 * v + 128].astype(F32)
        packed[2 * v] = jnp.where(left_half, o, pltpu.roll(a, 64, 1)).astype(BF)
        packed[2 * v + 1] = jnp.where(left_half, pltpu.roll(o, 64, 1), a).astype(BF)

    @pl.when(is_worker)
    def _():
        pltpu.make_async_copy(packed.at[slot], data_in.at[chip], recv_sem.at[1]).start()

    for turn in range(4):

        @pl.when(x == turn)
        def _():
            turned = tuple((w + 4 * turn) % 16 for w in range(16))
            send_all(lambda w: packed.at[w], data_in.at[chip], 1, turned)

    def await_bytes(ref, sem):
        pltpu.make_async_copy(ref, ref, sem).wait()

    @pl.when(is_worker)
    def _():
        await_bytes(meta_in, recv_sem.at[0])
        block = lax.broadcasted_iota(I32, (8, 128), 1) // 32
        for f in range(16):
            turned = meta_in[0:8, 0, f // 4 * 128 : f // 4 * 128 + 128]
            for q in range(1, 4):
                source = meta_in[8 * q : 8 * q + 8, 0, f // 4 * 128 : f // 4 * 128 + 128]
                turned = jnp.where(block == (q + f % 4) % 4, source, turned)
            turned = pltpu.roll(turned, (4 - f % 4) * 32, 1) if f % 4 else turned
            meta_turn[f] = turned
        meta = jnp.concatenate([meta_turn[:, group, :] for group in range(8)], axis=1)
        position = meta[14:15] * 32.0 + meta[15:16] - 1.0
        part_row = lax.broadcasted_iota(I32, (16, 1024), 0)
        right = jnp.where(part_row < 11, meta, jnp.where(part_row < 14, 1.0, 0.0)).astype(BF)
        shift = jnp.concatenate([meta[13:16], meta[0:13]], axis=0)
        raised = jnp.where(
            part_row < 8, -2.0 * meta, jnp.where((part_row >= 11) & (part_row < 14), shift, 0.0)
        )
        raised = jnp.where(part_row == 14, meta[11:12], raised).astype(BF)
        factor = jnp.where(part_row == 14, meta[13:14], jnp.where(part_row == 15, meta[12:13], 0.0)).astype(BF)

        eight = jnp.concatenate([raised] * 8, axis=0)
        chunk_lane = lax.broadcasted_iota(I32, (64, 128), 1) // 16
        gathered = [None, None]
        swaps = [None, None]
        for k in (1, 0):
            half = core if k else 1 - core
            for chunk in range(4 * k, 4 * k + 4):
                line = lax.broadcasted_iota(I32, (64, 1), 0) + 64 * (chunk % 4)
                order = line // 32 * 64 + half * 32 + line % 32
                hit = (position == order.astype(F32)).astype(BF)
                pick[pl.ds(64 * chunk, 64), :] = hit
            picked = lax.dot_general(
                pick[256 * k : 256 * k + 256], eight, (((1,), (1,)), ((), ())), preferred_element_type=F32
            )
            gathered[k] = total(
                [jnp.where(chunk_lane == 4 * k + g, picked[64 * g : 64 * g + 64], 0.0) for g in range(4)]
            )
            lift[1 - k] = pltpu.roll(gathered[k], 64, 1).astype(BF)
            swaps[1 - k] = pltpu.make_async_remote_copy(
                src_ref=lift.at[1 - k], dst_ref=lift_in.at[1 - k],
                send_sem=pair_sem.at[6 - 6 * k], recv_sem=pair_sem.at[7 - 6 * k],
                device_id=peer, device_id_type=MESH,
            )
            swaps[1 - k].start()
        right = jnp.concatenate([right] * 8, axis=0)
        factor = jnp.concatenate([factor] * 8, axis=0)
        spread = lax.broadcasted_iota(I32, (64, 128), 1) % 16
        ones = jnp.where(((spread >= 8) & (spread < 11)) | (spread == 15), 1.0, 0.0)

        def selected(k):
            swaps[k].wait_recv()
            return gathered[k] + lift_in[k].astype(F32) + ones

        scale = -kernel_rate * math.log2(math.e)

        def form(chunk, left):
            rows = slice(64 * chunk, 64 * chunk + 64)
            one = jnp.where(chunk_lane == chunk, left, 0.0).astype(BF)
            distance = jnp.dot(one, right, preferred_element_type=F32)
            coef = jnp.dot(one, factor, preferred_element_type=F32)
            diagonal = pick[rows, :].astype(F32)
            entry = (jnp.exp2(distance * scale) + diagonal).astype(BF)
            mat[rows, :] = entry * coef.astype(BF)

        left_lanes = lax.broadcasted_iota(I32, (8, 16, 128), 2) < 64

        def combine(first, count):
            rows = slice(first, first + 32 * count)
            data = data_in[...].reshape(1024, 128)
            chosen = jnp.dot(pick[rows], data, preferred_element_type=F32).reshape(count, 32, 128)
            product = jnp.dot(mat[rows], data, preferred_element_type=F32).reshape(count, 32, 128)
            above = pltpu.roll(chosen[:, 0:16], 64, 2) - product[:, 0:16]
            below = chosen[:, 16:32] - pltpu.roll(product[:, 16:32], 64, 2)
            return jnp.where(left_lanes[0:count], above, below)

        left = selected(0)
        for chunk in range(4):
            form(chunk, left)
        await_bytes(data_in, recv_sem.at[1])
        trades = []
        for k in range(2):
            part[4 * k : 4 * k + 4] = combine(128 * k, 4)
            trade = pltpu.make_async_remote_copy(
                src_ref=part.at[pl.ds(4 * k, 4)], dst_ref=part_in.at[pl.ds(4 * k, 4)],
                send_sem=pair_sem.at[2 + 2 * k], recv_sem=pair_sem.at[3 + 2 * k],
                device_id=peer, device_id_type=MESH,
            )
            trade.start()
            trades.append(trade)
        left = selected(1)
        for chunk in range(4, 8):
            form(chunk, left)
        mine_rows = combine(256, 8)
        last_rank = rank_s[2, leaf]
        order = (
            lax.broadcasted_iota(I32, (8, 16, 128), 0) * 64 + core * 32
            + jnp.where(left_lanes, 0, 16) + lax.broadcasted_iota(I32, (8, 16, 128), 1)
        )
        for k in range(2):
            trades[k].wait_recv()
            these = slice(4 * k, 4 * k + 4)
            blocks[these] = jnp.where(order[these] < last_rank, mine_rows[these] + part_in[these], 0.0).astype(BF)
            for number in OUT_ORDER[k]:
                block = blocks.at[number % 8]

                @pl.when(chip != number)
                def _():
                    pltpu.make_async_remote_copy(
                        src_ref=block,
                        dst_ref=pieces.at[slot],
                        send_sem=send_sem.at[2],
                        recv_sem=recv_sem.at[2],
                        device_id=device(number),
                        device_id_type=MESH,
                    ).start()

        pltpu.make_async_copy(blocks.at[x * 2 + y], pieces.at[slot], recv_sem.at[2]).start()

    await_bytes(pieces, recv_sem.at[2])
    left_part = lax.broadcasted_iota(I32, (16, 128), 1) < 64
    for v in range(8):
        even = pieces[2 * v].astype(F32)
        odd = pieces[2 * v + 1].astype(F32)
        columns = slice(128 * v, 128 * v + 128)
        out[0, 0:16, columns] = jnp.where(left_part, even, pltpu.roll(odd, 64, 1)).astype(BF)
        out[0, 16:32, columns] = jnp.where(left_part, pltpu.roll(even, 64, 1), odd).astype(BF)

    @pl.when(is_worker)
    def _():
        for k in range(2):
            pltpu.make_async_copy(lift.at[k], lift_in.at[k], pair_sem.at[6 * k]).wait()
        for k in range(2):
            pltpu.make_async_copy(part.at[pl.ds(4 * k, 4)], part_in.at[pl.ds(4 * k, 4)], pair_sem.at[2 + 2 * k]).wait()
        await_bytes(data_in.at[pl.ds(0, 31), pl.ds(0, 16)], send_sem.at[2])
        await_bytes(meta_in.at[pl.ds(0, 15)], send_sem.at[0])
        await_bytes(data_in.at[pl.ds(0, 15)], send_sem.at[1])

    @pl.when(jnp.logical_not(is_worker))
    def _():
        await_bytes(meta_in.at[pl.ds(0, 16)], send_sem.at[0])
        await_bytes(data_in.at[pl.ds(0, 16)], send_sem.at[1])


def body(samples, omega, points, ranks, pivots):
    anywhere = pl.BlockSpec(memory_space=pl.ANY)
    return pl.pallas_call(
        kernel,
        out_shape=pltpu.VMEM((1, 32, 1024), BF),
        in_specs=[anywhere] * 5,
        out_specs=pl.BlockSpec(memory_space=pltpu.VMEM),
        scratch_shapes=[
            pltpu.VMEM((8, 32), BF),
            pltpu.VMEM((2, 1, 512), I32),
            pltpu.SMEM((3, 32), I32),
            pltpu.VMEM((32, 1024), BF),
            pltpu.VMEM((32, 1024), BF),
            pltpu.VMEM((16, 32, 128), BF),
            pltpu.VMEM((1, 512), F32),
            pltpu.VMEM((32, 1, 512), F32),
            pltpu.VMEM((16, 8, 128), F32),
            pltpu.VMEM((32, 32, 128), BF),
            pltpu.VMEM((512, 1024), BF),
            pltpu.VMEM((512, 1024), BF),
            pltpu.VMEM((2, 64, 128), BF),
            pltpu.VMEM((2, 64, 128), BF),
            pltpu.VMEM((8, 16, 128), F32),
            pltpu.VMEM((8, 16, 128), F32),
            pltpu.VMEM((8, 16, 128), BF),
            pltpu.VMEM((16, 16, 128), BF),
            pltpu.SemaphoreType.DMA((5,)),
            pltpu.SemaphoreType.DMA((3,)),
            pltpu.SemaphoreType.DMA((3,)),
            pltpu.SemaphoreType.DMA((8,)),
        ],
        compiler_params=pltpu.CompilerParams(
            collective_id=0, has_side_effects=True, vmem_limit_bytes=60 * 2**20
        ),
        cost_estimate=pl.CostEstimate(flops=300_000_000, bytes_accessed=200_000, transcendentals=524288),
    )(samples, omega, points[:, 0, :], ranks, pivots)


def solution(mesh):
    return jax.shard_map(
        body,
        mesh=mesh,
        in_specs=(
            P("leaf", "grid", None),
            P("leaf", "grid", None),
            P(None, "leaf", "grid"),
            P(),
            P(None, "leaf", None),
        ),
        out_specs=P("leaf", "grid", None),
        check_vma=False,
    )
```
